256 devices in a mesh: dp: 8 (over y, core), ctx: 32 (over z, x).
Axes of the slice: x: 4, y: 4, z: 8, core: 2. Of those that a mesh axis runs over, the one named last changes fastest.
Arguments:
- text_rows: bfloat16 [8, 4096, 5120], P('dp', 'ctx'), may hold values from -5 to 5
- image_rows: bfloat16 [8, 256, 5120], P('dp', 'ctx'), may hold values from -5 to 5
- tile_counts: int32 [8, 32], P('dp', 'ctx'), may hold values from 1 to 8, as said below
- tile_offsets: int32 [8, 32], P('dp', 'ctx'), may hold values from 0 to 4088, as said below
- doc_ids: int32 [8, 4096], P('dp', 'ctx'), may hold values from 0 to 7, never falling along the last dimension, each value on 1 to 2176 neighbouring positions
- out_grad: bfloat16 [8, 4096, 4096], P('dp', 'ctx'), may hold values from -6 to 6
- proj_scale: float32 [5120], replicated, may hold values from 0.5 to 1.5
- proj_shift: float32 [5120], replicated, may hold values from -3 to 3
Outputs:
- attn_out: bfloat16 [8, 4096, 4096], P('dp', 'ctx')
- text_grad: bfloat16 [8, 4096, 5120], P('dp', 'ctx')
- image_grad: bfloat16 [8, 256, 5120], P('dp', 'ctx')
- scale_grad: float32 [5120], replicated
- shift_grad: float32 [5120], replicated
The draws below stay inside these ranges and needn't reach their ends.
Inputs may be any that keep to these rules, and one draw needn't show every extreme that they name: `tile_counts`: in every sequence one owner's count is exactly 8. The images of one sequence do not intersect and end within the sequence: tile_offsets + tile_counts <= 4096; in every sequence one image ends exactly at position 4096.
All inputs are finite; a program needn't handle non-finite values.
Results may differ from the reference program's by a relative error of at most 0.02.
Values may be sent and summed in bfloat16 or wider, within the bound.
A program may use at most 64 MiB of HBM per device.

```python
import math
import jax
import jax.numpy as jnp
import numpy as np
from jax import lax

HD = 128
HEADS = 32
KVH = 4
TOK_DEV = 128
SLOTS = 8
DOCS = 8
QW = 5120
SEQ = 4096
DOC_MOST = 2176
N_DP = 8
N_CTX = 32


def tile_layout(key):
    key_count, key_gap, key_order, key_full = jax.random.split(key, 4)
    counts = jax.random.randint(key_count, (N_DP, N_CTX), 1, SLOTS + 1)
    full_owner = jax.random.randint(key_full, (N_DP, 1), 0, N_CTX)
    owners = jnp.arange(N_CTX, dtype=jnp.int32)[None, :]
    counts = jnp.where(owners == full_owner, SLOTS, counts).astype(jnp.int32)
    gaps = jax.random.randint(key_gap, (N_DP, N_CTX), 0, TOK_DEV - SLOTS + 1)
    ranking = jax.random.randint(key_order, (N_DP, N_CTX), 0, 1 << 20) * N_CTX + owners
    ranking = jnp.where(owners == full_owner, (1 << 20) * N_CTX + owners, ranking)
    order = jnp.argsort(ranking, axis=1)
    ordered = jnp.take_along_axis(counts, order, axis=1)
    ends = jnp.cumsum(gaps + ordered, axis=1)
    begins = (ends - ordered).astype(jnp.int32)
    begins = begins.at[:, N_CTX - 1].set(SEQ - SLOTS)
    offsets = jnp.zeros((N_DP, N_CTX), jnp.int32).at[jnp.arange(N_DP)[:, None], order].set(begins)
    return (counts, offsets)


def draw_tile_counts(key, part):
    return tile_layout(key)[0]


def draw_tile_offsets(key, part):
    return tile_layout(key)[1]


def draw_text_rows(key, part):
    key = jax.random.fold_in(key, 7)
    key_base = jax.random.fold_in(key, 0)
    values = jnp.clip(jax.random.normal(key_base, (N_DP, SEQ, QW), jnp.float32), -4.5, 4.5)
    return values.astype(jnp.bfloat16)


def levels(own_key, dims, cuts, low, top_value):
    def one(position, shards_of):
        steps = jax.random.uniform(jax.random.fold_in(jax.random.fold_in(own_key, 6), position), (shards_of,), jnp.float32, low / len(cuts), top_value / len(cuts))
        return jnp.repeat(jnp.exp(steps), dims[position] // shards_of).reshape((-1,) + (1,) * (len(dims) - position - 1))

    gain = one(*cuts[0])
    for cut in cuts[1:]:
        gain = gain * one(*cut)
    return gain


def split_up(number_of, total, reach, lean):
    loads = [(1 << 20) // math.isqrt(grade ** lean) + 1 for grade in range(2, number_of + 1)]
    rest, given = total - reach - (number_of - 1), [1] * (number_of - 1)
    while rest > 0:
        free = [i for i in range(number_of - 1) if given[i] < reach]
        pool, budget = sum([loads[i] for i in free]), rest
        for i in free:
            extra = min(reach - given[i], max(1, budget * loads[i] // pool), rest)
            given[i] = given[i] + extra
            rest = rest - extra
    return np.array([reach] + given)


def ragged_sizes(rng, count, total, reach, slope):
    if count == 2:
        one = jax.random.randint(rng, (), max(1, total - reach), min(reach, total - 1) + 1)
        return jnp.stack([one, total - one])
    lengths = jnp.asarray(split_up(count, total, reach, slope), jnp.int32)
    twos = (count - 1) // 2
    source_of, sink = lengths[1:1 + 2 * twos:2], lengths[2:2 + 2 * twos:2]
    slack = jnp.minimum(source_of - 1, reach - sink)
    passed = jax.random.randint(jax.random.fold_in(rng, 1), (twos,), 0, 1 << 20) % (slack + 1)
    lengths = lengths.at[1:1 + 2 * twos:2].set(source_of - passed).at[2:2 + 2 * twos:2].set(sink + passed)
    return lengths[jax.random.permutation(jax.random.fold_in(rng, 2), count)]


def noise(stream_key, shape, spread, most, cuts=(), kind=jnp.bfloat16):
    loudness = levels(stream_key, shape, cuts, -0.22, 0.18) if cuts else 1.0
    entries = jax.random.normal(stream_key, shape, jnp.float32) * spread * loudness
    return jnp.minimum(jnp.maximum(entries, -most), most).astype(kind)


def setup_inputs(seed: int = 0) -> dict:
    streams_of = jax.random.split(jax.random.key(seed), 9)
    return {
        "text_rows": draw_text_rows(jax.random.fold_in(streams_of[8], 71), 0),
        "image_rows": noise(streams_of[1], (N_DP, N_CTX * SLOTS, QW), 1.0, 5.0, ((0, 8), (1, 32))),
        "tile_counts": draw_tile_counts(jax.random.fold_in(streams_of[8], 71), 0),
        "tile_offsets": draw_tile_offsets(jax.random.fold_in(streams_of[8], 71), 0),
        "doc_ids": jax.vmap(lambda own: jnp.searchsorted(jnp.cumsum(ragged_sizes(own, DOCS, SEQ, DOC_MOST, 0)), jnp.arange(SEQ), side="right"))(jax.random.split(streams_of[4], N_DP)).reshape((N_DP, SEQ)).astype(jnp.int32),
        "out_grad": noise(streams_of[5], (N_DP, SEQ, HEADS * HD), 1.0, 6.0, ((0, 8), (1, 32))),
        "proj_scale": jnp.clip(1.0 + 0.1 * jax.random.normal(streams_of[6], (QW,), jnp.float32), 0.5, 1.5),
        "proj_shift": noise(streams_of[7], (QW,), 0.5, 3.0, (), jnp.float32),
    }


def one_sequence(text, image, counts, offsets, docs, dout, proj_scale, proj_shift):
    rep = HEADS // KVH
    qwidth = HEADS * HD
    score_scale = HD ** -0.5
    adapted = (image.astype(jnp.float32) * proj_scale + proj_shift).astype(jnp.bfloat16)
    positions = jnp.arange(SEQ, dtype=jnp.int32)
    owners = jnp.arange(N_CTX, dtype=jnp.int32)
    covered = (positions[:, None] >= offsets[None, :]) & (positions[:, None] < (offsets + counts)[None, :])
    is_image = jnp.any(covered, axis=1)
    owner_of = jnp.sum(jnp.where(covered, owners[None, :], 0), axis=1)
    first_of = jnp.sum(jnp.where(covered, offsets[None, :], 0), axis=1)
    slot_of = jnp.where(is_image, owner_of * SLOTS + positions - first_of, 0).astype(jnp.int32)
    rows = jnp.where(is_image[:, None], jnp.take(adapted, slot_of, axis=0), text)
    query = rows[:, :qwidth].reshape(SEQ, KVH, rep, HD)
    keys = rows[:, qwidth:qwidth + KVH * HD].reshape(SEQ, KVH, HD).astype(jnp.float32)
    vals = rows[:, qwidth + KVH * HD:].reshape(SEQ, KVH, HD).astype(jnp.float32)
    match = docs[:, None] == jnp.arange(DOCS, dtype=jnp.int32)[None, :]
    totals = jnp.sum(match.astype(jnp.int32), axis=0)
    before = jnp.cumsum(totals) - totals
    doc_start = jnp.sum(jnp.where(match, before[None, :], 0), axis=1).astype(jnp.int32)
    dout_r = dout.reshape(SEQ, KVH, rep, HD)

    def block(carry, index):
        begin = (index * TOK_DEV).astype(jnp.int32)
        qblock = lax.dynamic_slice_in_dim(query, begin, TOK_DEV, 0).astype(jnp.float32)
        dblock = lax.dynamic_slice_in_dim(dout_r, begin, TOK_DEV, 0).astype(jnp.float32)
        qpos = begin + jnp.arange(TOK_DEV, dtype=jnp.int32)
        qstart = lax.dynamic_slice_in_dim(doc_start, begin, TOK_DEV, 0)
        allowed = (positions[None, :] <= qpos[:, None]) & (positions[None, :] >= qstart[:, None])
        allowed = allowed[None, None]
        scores = jnp.einsum('pgrd,tgd->grpt', qblock, keys) * score_scale
        row_max = jnp.max(jnp.where(allowed, scores, -1e30), axis=-1)
        expd = jnp.where(allowed, jnp.exp(scores - row_max[..., None]), 0.0)
        row_total = jnp.sum(expd, axis=-1)
        weights = expd.astype(jnp.bfloat16).astype(jnp.float32)
        attn = (jnp.einsum('grpt,tgd->grpd', weights, vals) / row_total[..., None]).astype(jnp.bfloat16)
        log_total = row_max + jnp.log(row_total)
        corr = jnp.einsum('pgrd,grpd->grp', dblock, attn.astype(jnp.float32))
        prob = jnp.where(allowed, jnp.exp(scores - log_total[..., None]), 0.0)
        prob_b = prob.astype(jnp.bfloat16).astype(jnp.float32)
        dprob = jnp.einsum('pgrd,tgd->grpt', dblock, vals)
        dscore = (prob * (dprob - corr[..., None]) * score_scale).astype(jnp.bfloat16).astype(jnp.float32)
        query_grad = jnp.einsum('grpt,tgd->grpd', dscore, keys).astype(jnp.bfloat16)
        key_part = jnp.einsum('grpt,pgrd->tgd', dscore, qblock).reshape(SEQ, KVH * HD)
        val_part = jnp.einsum('grpt,pgrd->tgd', prob_b, dblock).reshape(SEQ, KVH * HD)
        part = jnp.concatenate([key_part, val_part], axis=1).astype(jnp.bfloat16)
        part = lax.optimization_barrier(part)
        return carry + part.astype(jnp.float32), (attn, query_grad)

    init = jnp.zeros((SEQ, 2 * KVH * HD), jnp.float32)
    keyval_sum, (attn_all, qgrad_all) = lax.scan(block, init, jnp.arange(N_CTX, dtype=jnp.int32))
    attn_out = attn_all.transpose(0, 3, 1, 2, 4).reshape(SEQ, qwidth)
    query_grad = qgrad_all.transpose(0, 3, 1, 2, 4).reshape(SEQ, qwidth)
    grad_rows = jnp.concatenate([query_grad, keyval_sum.astype(jnp.bfloat16)], axis=1)
    text_grad = jnp.where(is_image[:, None], jnp.zeros_like(grad_rows), grad_rows)
    slots = jnp.arange(N_CTX * SLOTS, dtype=jnp.int32)
    slot_owner = slots // SLOTS
    within = slots % SLOTS
    live = within < counts[slot_owner]
    target = jnp.clip(offsets[slot_owner] + within, 0, SEQ - 1).astype(jnp.int32)
    adapted_grad = jnp.where(live[:, None], jnp.take(grad_rows, target, axis=0), jnp.zeros((), jnp.bfloat16))
    grad_f = adapted_grad.astype(jnp.float32)
    image_grad = (grad_f * proj_scale).astype(jnp.bfloat16)
    scale_part = jnp.sum(grad_f * image.astype(jnp.float32), axis=0)
    shift_part = jnp.sum(grad_f, axis=0)
    return attn_out, text_grad, image_grad, scale_part, shift_part


def reference(text_rows, image_rows, tile_counts, tile_offsets, doc_ids, out_grad, proj_scale, proj_shift):
    def run(items):
        return one_sequence(items[0], items[1], items[2], items[3], items[4], items[5], proj_scale, proj_shift)

    attn_out, text_grad, image_grad, scale_parts, shift_parts = lax.map(
        run, (text_rows, image_rows, tile_counts, tile_offsets, doc_ids, out_grad))
    return attn_out, text_grad, image_grad, jnp.sum(scale_parts, axis=0), jnp.sum(shift_parts, axis=0)
```

```python
import math

import jax
import jax.numpy as jnp
from jax import lax
from jax.experimental import pallas as pl
from jax.experimental.pallas import tpu as pltpu
from jax.sharding import PartitionSpec as P

MESH = pl.DeviceIdType.MESH
HD = 128
REP = 8
DOCS = 8
NZ = 8
NX = 4
NDP = 8
TOK = 128
ROW = NX * TOK
SLOTS = 8
NSLOT = NZ * NX * SLOTS
QC = REP * HD
HC = QC + 2 * HD
WIN = 6
HALF = HC // 2
SCALE = HD ** -0.5
LOG2E = math.log2(math.e)
F32 = jnp.float32
BF16 = jnp.bfloat16
NT = (((1,), (1,)), ((), ()))


def place():
    ctx = lax.axis_index("ctx")
    return lax.axis_index("dp"), ctx // NX, ctx % NX


def ctx_of(z, x):
    return {"ctx": z * NX + x}


def remote(src, dst, send, recv, device):
    return pltpu.make_async_remote_copy(
        src_ref=src, dst_ref=dst, send_sem=send, recv_sem=recv, device_id=device, device_id_type=MESH
    )


def cols(start, size):
    return pl.ds(pl.multiple_of(start, HD), size)


def rows_of(start, size):
    return pl.ds(pl.multiple_of(start, size), size)


def greet(devices):
    barrier = pltpu.get_barrier_semaphore()
    for device in devices:
        pl.semaphore_signal(barrier, inc=1, device_id=device, device_id_type=MESH)
    pl.semaphore_wait(barrier, len(devices))


def spread_kernel(
    text, dout, image, meta, q, do, kvw, images, metas,
    own_sem, x_send, x_recv, kv_send, kv_recv, up_send, up_recv, down_send, down_recv,
):
    _, z, x = place()
    up, down = (z + 1) % NZ, (z + NZ - 1) % NZ
    me = z * NX + x
    greet([ctx_of(z, (x + d) % NX) for d in (1, 2, 3)] + [ctx_of(up, x), ctx_of(down, x)])

    def pieces(head):
        return [
            (meta, metas.at[me]),
            (image.at[head], images.at[me]),
            (text.at[:, cols(NX * QC + head * HD, HD)], kvw.at[WIN - 1, rows_of(x * TOK, TOK), pl.ds(0, HD)]),
            (text.at[:, cols(NX * QC + (NX + head) * HD, HD)], kvw.at[WIN - 1, rows_of(x * TOK, TOK), pl.ds(HD, HD)]),
            (text.at[:, cols(head * QC, QC)], q.at[rows_of(x * TOK, TOK)]),
            (dout.at[:, cols(head * QC, QC)], do.at[rows_of(x * TOK, TOK)]),
        ]

    own = [pltpu.make_async_copy(src, dst, own_sem.at[k]) for k, (src, dst) in enumerate(pieces(x))]
    sent = []
    for d in (1, 2, 3):
        peer = (x + d) % NX
        sent.append([
            remote(src, dst, x_send.at[d - 1, k], x_recv.at[d - 1, k], ctx_of(z, peer))
            for k, (src, dst) in enumerate(pieces(peer))
        ])
    for k in range(6):
        own[k].start()
        for d in range(3):
            sent[d][k].start()

    def arrived(k):
        own[k].wait()
        for d in range(3):
            sent[d][k].wait_recv()

    ups, downs, kvs = [], [], []
    for k in range(4):
        block = pl.ds(((z + NZ - k) % NZ) * NX, NX)
        ups.append([
            remote(a.at[block], a.at[block], up_send.at[k, j], up_recv.at[k, j], ctx_of(up, x))
            for j, a in enumerate((metas, images))
        ])
    for k in range(3):
        block = pl.ds(((z + k) % NZ) * NX, NX)
        downs.append([
            remote(a.at[block], a.at[block], down_send.at[k, j], down_recv.at[k, j], ctx_of(down, x))
            for j, a in enumerate((metas, images))
        ])
    for k in range(5):
        part = pl.ds(0, ROW) if k < 4 else pl.ds(ROW - TOK, TOK)
        kvs.append(
            remote(kvw.at[WIN - 1 - k, part], kvw.at[WIN - 2 - k, part], kv_send.at[k], kv_recv.at[k], ctx_of(up, x))
        )

    arrived(2)
    arrived(3)

    @pl.when(z <= NZ - 2)
    def _():
        kvs[0].start()

    arrived(0)
    arrived(1)
    for j in range(2):
        ups[0][j].start()
        downs[0][j].start()
    for k in range(1, 5):

        @pl.when(z >= k)
        def _():
            kvs[k - 1].wait_recv()

        @pl.when((z >= k) & (z <= NZ - 2))
        def _():
            kvs[k].start()

        for j in range(2):
            ups[k - 1][j].wait_recv()
            if k < 4:
                ups[k][j].start()
        if k <= 3:
            for j in range(2):
                downs[k - 1][j].wait_recv()
                if k < 3:
                    downs[k][j].start()

    @pl.when(z >= 5)
    def _():
        kvs[4].wait_recv()

    arrived(4)
    arrived(5)
    for k in range(5):

        @pl.when((z >= k) & (z <= NZ - 2))
        def _():
            kvs[k].wait_send()

    for group in sent + ups + downs:
        for copy in group:
            copy.wait_send()


def attend_kernel(
    q, do, kvw, images, docs, tgt_row, tgt_col, proj,
    attn, dqm, dkv_out, scatq, sums, onehot_t, keep, rawkv,
    raw, adapted, qm, dq, ks, vs, kts, vts, s_buf, p_buf, o_acc, dkv,
):
    _, z, x = place()
    base = z * ROW
    scale = proj[pl.ds(x, 1), :]
    shift = proj[pl.ds(NX + x, 1), :]
    for pair in range(NSLOT // 16):
        first = images[2 * pair].astype(F32)
        second = images[2 * pair + 1].astype(F32)
        left = jnp.concatenate([first[:8], second[:8]], axis=0)
        right = jnp.concatenate([first[8:], second[8:]], axis=0)
        at = pl.ds(pair * 16, 16)
        raw[at, pl.ds(0, HALF)] = left.astype(BF16)
        raw[at, pl.ds(HALF, HALF)] = right.astype(BF16)
        adapted[at, pl.ds(0, HALF)] = (left * scale[:, :HALF] + shift[:, :HALF]).astype(BF16)
        adapted[at, pl.ds(HALF, HALF)] = (right * scale[:, HALF:] + shift[:, HALF:]).astype(BF16)
    rawkv[...] = raw[:, QC:]

    target = tgt_row[...]

    def chosen(begin):
        position = begin + lax.broadcasted_iota(jnp.int32, (ROW, NSLOT), 0)
        hit = jnp.where(position == target, 1.0, 0.0).astype(F32)
        return hit.astype(BF16), jnp.max(hit, axis=1, keepdims=True)

    hit, is_image = chosen(base)
    keep[...] = jnp.broadcast_to(1.0 - is_image, keep.shape)
    onehot_t[...] = jnp.where(
        tgt_col[...] == base + lax.broadcasted_iota(jnp.int32, (NSLOT, ROW), 1), 1.0, 0.0
    ).astype(BF16)
    picked = jnp.dot(hit, adapted[:, :QC], preferred_element_type=F32)
    qm[...] = jnp.where(is_image > 0.0, picked, q[...].astype(F32)).astype(BF16)

    all_docs = docs[...]
    own_docs = docs[pl.ds(z * NX, NX), :]
    own_docs = jnp.concatenate([own_docs[k : k + 1] for k in range(NX)], axis=1)
    doc_start = jnp.zeros((1, ROW), jnp.int32)
    for doc in range(1, DOCS):
        before = jnp.sum((all_docs < doc).astype(jnp.int32))
        doc_start = jnp.where(own_docs == doc, before, doc_start)
    first_key = jnp.min(doc_start)
    low = jnp.maximum((first_key - (base - (WIN - 1) * ROW)) // ROW, 0)
    low = jnp.maximum(low, WIN - 1 - z)

    dkv[...] = jnp.zeros_like(dkv)

    def place_keys(s, _):
        hit, is_image = chosen(base + (s - (WIN - 1)) * ROW)
        picked = jnp.dot(hit, adapted[:, QC:], preferred_element_type=F32)
        old = kvw[s].astype(F32)
        if True:
            live = (s > 0) | (lax.broadcasted_iota(jnp.int32, (ROW, 1), 0) >= ROW - TOK)
            old = jnp.where(live, old, 0.0)
        both = jnp.where(is_image > 0.0, picked, old)
        ks[s] = both[:, :HD].astype(BF16)
        vs[s] = both[:, HD:].astype(BF16)
        kts[s] = both[:, :HD].T.astype(BF16)
        vts[s] = both[:, HD:].T.astype(BF16)
        return 0

    lax.fori_loop(low, WIN, place_keys, 0)

    query_pos = base + lax.broadcasted_iota(jnp.int32, (1, ROW), 1)

    def head(r, _):
        at = cols(r * HD, HD)
        q_t = qm[:, at].astype(F32).T
        do_t = do[:, at].astype(F32).T
        q_tb = q_t.astype(BF16)
        do_tb = do_t.astype(BF16)

        def scores(s, top):
            key_pos = base + (s - (WIN - 1)) * ROW + lax.broadcasted_iota(jnp.int32, (ROW, 1), 0)
            value = jnp.dot(ks[s], q_tb, preferred_element_type=F32) * (SCALE * LOG2E)
            value = jnp.where((key_pos >= doc_start) & (key_pos <= query_pos), value, -1e30)
            s_buf[s] = value
            return jnp.maximum(top, jnp.max(value.reshape(ROW // 8, 8, ROW), axis=0))

        top = lax.fori_loop(low, WIN, scores, jnp.full((8, ROW), -1e30, F32))
        top = jnp.max(top, axis=0, keepdims=True)
        o_acc[...] = jnp.zeros_like(o_acc)

        def weigh(s, total):
            value = jnp.exp2(s_buf[s] - top)
            value_b = value.astype(BF16)
            p_buf[s] = value_b
            o_acc[...] += jnp.dot(vts[s], value_b, preferred_element_type=F32)
            return total + jnp.sum(value.reshape(ROW // 8, 8, ROW), axis=0)

        total = lax.fori_loop(low, WIN, weigh, jnp.zeros((8, ROW), F32))
        inverse = 1.0 / jnp.sum(total, axis=0, keepdims=True)
        out_t = (o_acc[...] * inverse).astype(BF16).astype(F32)
        attn[:, at] = out_t.T.astype(BF16)
        corr = jnp.sum(do_t * out_t, axis=0, keepdims=True)
        q_n = (q_t * (inverse * SCALE)).T.astype(BF16)
        do_n = (do_t * inverse).T.astype(BF16)
        o_acc[...] = jnp.zeros_like(o_acc)

        def back(s, _):
            prob = p_buf[s]
            dprob = jnp.dot(vs[s], do_tb, preferred_element_type=F32)
            dscore = (prob.astype(F32) * (dprob - corr)).astype(BF16)
            o_acc[...] += jnp.dot(kts[s], dscore, preferred_element_type=F32)
            dkv[s, :, :HD] += jnp.dot(dscore, q_n, preferred_element_type=F32)
            dkv[s, :, HD:] += jnp.dot(prob, do_n, preferred_element_type=F32)
            return 0

        lax.fori_loop(low, WIN, back, 0)
        dq[:, at] = (o_acc[...] * (inverse * SCALE)).T.astype(BF16)
        return 0

    lax.fori_loop(0, REP, head, 0)

    dkv_out[...] = dkv[...].astype(BF16)
    dqm[...] = jnp.where(is_image > 0.0, 0.0, dq[...].astype(F32)).astype(BF16)
    scattered = jnp.dot(onehot_t[...], dq[...], preferred_element_type=F32)
    scatq[...] = scattered.astype(BF16)
    scale_part = jnp.sum(scattered * raw[:, :QC].astype(F32), axis=0, keepdims=True)
    shift_part = jnp.sum(scattered, axis=0, keepdims=True)
    sums[...] = jnp.zeros_like(sums)
    for k in range(REP):
        sums[pl.ds(k, 1), :] = scale_part[:, k * HD : (k + 1) * HD]
        sums[pl.ds(10 + k, 1), :] = shift_part[:, k * HD : (k + 1) * HD]


def return_kernel(
    attn, dqm, part, scatq, sums_in, onehot_t, keep, rawkv, proj,
    attn_out, text_grad, image_out, sums_out,
    first_in, ring_in, ring_out, dkv, mkv, scatkv, rxq, rxkv, igs, vec, vec_z, vec_x, r_dp, r_z, r_x,
    own_sem, x_send, x_recv, ring_send, ring_recv, z_send, z_recv, dp_send, dp_recv,
):
    dp, z, x = place()
    up, down = (z + 1) % NZ, (z + NZ - 1) % NZ
    greet(
        [ctx_of(z, (x + d) % NX) for d in (1, 2, 3)]
        + [ctx_of((z + d) % NZ, x) for d in range(1, NZ)]
        + [{"dp": (dp + d) % NDP} for d in range(1, NDP)]
    )

    head = remote(
        part.at[0, pl.ds(ROW - TOK, TOK)], first_in, ring_send.at[0], ring_recv.at[0], ctx_of(down, x)
    )

    @pl.when(z >= WIN - 1)
    def _():
        head.start()

    def row_pieces(peer):
        return [
            (attn.at[rows_of(peer * TOK, TOK)], attn_out.at[:, cols(x * QC, QC)]),
            (dqm.at[rows_of(peer * TOK, TOK)], text_grad.at[:, cols(x * QC, QC)]),
            (mkv.at[rows_of(peer * TOK, TOK), pl.ds(0, HD)], text_grad.at[:, cols(NX * QC + x * HD, HD)]),
            (mkv.at[rows_of(peer * TOK, TOK), pl.ds(HD, HD)], text_grad.at[:, cols(NX * QC + (NX + x) * HD, HD)]),
            (igs.at[peer], image_out.at[x]),
            (vec_x, r_x.at[x]),
        ]

    own = [pltpu.make_async_copy(src, dst, own_sem.at[k]) for k, (src, dst) in enumerate(row_pieces(x))]
    sent = []
    for d in (1, 2, 3):
        peer = (x + d) % NX
        sent.append([
            remote(src, dst, x_send.at[d - 1, k], x_recv.at[d - 1, k], ctx_of(z, peer))
            for k, (src, dst) in enumerate(row_pieces(peer))
        ])

    def send_x(k):
        for d in range(3):
            sent[d][k].start()
        own[k].start()

    def arrived_x(k):
        own[k].wait()
        for d in range(3):
            sent[d][k].wait_recv()

    def z_pieces(peer):
        return [
            (scatq.at[rows_of(peer * 32, 32)], rxq.at[z]),
            (scatkv.at[rows_of(peer * 32, 32)], rxkv.at[z]),
            (vec_z, r_z.at[z]),
        ]

    own_z = [pltpu.make_async_copy(src, dst, own_sem.at[6 + k]) for k, (src, dst) in enumerate(z_pieces(z))]
    sent_z = []
    for d in range(1, NZ):
        peer = (z + d) % NZ
        sent_z.append([
            remote(src, dst, z_send.at[d - 1, k], z_recv.at[d - 1, k], ctx_of(peer, x))
            for k, (src, dst) in enumerate(z_pieces(peer))
        ])

    def send_z(k):
        for d in range(NZ - 1):
            sent_z[d][k].start()
        own_z[k].start()

    def arrived_z(k):
        own_z[k].wait()
        for d in range(NZ - 1):
            sent_z[d][k].wait_recv()

    send_x(0)
    send_x(1)
    send_z(0)

    ring = [
        remote(ring_out.at[k], ring_in.at[k], ring_send.at[1 + k], ring_recv.at[1 + k], ctx_of(down, x))
        for k in range(4)
    ]
    for s in range(1, WIN - 1):

        @pl.when(z >= WIN - 1 - s)
        def _():
            @pl.when(z == NZ - 1)
            def _():
                ring_out[s - 1] = part[s]

            @pl.when(z <= NZ - 2)
            def _():
                if s == 1:
                    head.wait_recv()
                    ring_out[0, : ROW - TOK] = part[s, : ROW - TOK]
                    ring_out[0, ROW - TOK :] = (
                        part[s, ROW - TOK :].astype(F32) + first_in[...].astype(F32)
                    ).astype(BF16)
                else:
                    ring[s - 2].wait_recv()
                    ring_out[s - 1] = (part[s].astype(F32) + ring_in[s - 2].astype(F32)).astype(BF16)

            ring[s - 1].start()

    @pl.when(z == NZ - 1)
    def _():
        dkv[...] = part[WIN - 1]

    @pl.when(z <= NZ - 2)
    def _():
        ring[3].wait_recv()
        dkv[...] = (part[WIN - 1].astype(F32) + ring_in[3].astype(F32)).astype(BF16)

    whole = dkv[...]
    kept = keep[...]
    mkv[...] = (whole.astype(F32) * jnp.concatenate([kept, kept], axis=1)).astype(BF16)
    send_x(2)
    send_x(3)
    scattered = jnp.dot(onehot_t[...], whole, preferred_element_type=F32)
    scatkv[...] = scattered.astype(BF16)
    send_z(1)
    scale_part = jnp.sum(scattered * rawkv[...].astype(F32), axis=0, keepdims=True)
    shift_part = jnp.sum(scattered, axis=0, keepdims=True)
    vec[...] = sums_in[...]
    for k in range(2):
        vec[pl.ds(REP + k, 1), :] = scale_part[:, k * HD : (k + 1) * HD]
        vec[pl.ds(10 + REP + k, 1), :] = shift_part[:, k * HD : (k + 1) * HD]
    own_dp = pltpu.make_async_copy(vec, r_dp.at[dp], own_sem.at[9])
    sent_dp = [
        remote(vec, r_dp.at[dp], dp_send.at[d - 1], dp_recv.at[d - 1], {"dp": (dp + d) % NDP}) for d in range(1, NDP)
    ]
    for copy in sent_dp:
        copy.start()
    own_dp.start()

    arrived_z(0)
    arrived_z(1)
    scale = proj[pl.ds(x, 1), :]
    slots_q = rxq[0].astype(F32)
    slots_kv = rxkv[0].astype(F32)
    for k in range(1, NZ):
        slots_q = slots_q + rxq[k].astype(F32)
        slots_kv = slots_kv + rxkv[k].astype(F32)
    grad = jnp.concatenate([slots_q, slots_kv], axis=1) * scale
    for k in range(NX):
        piece = grad[k * SLOTS : (k + 1) * SLOTS]
        igs[k] = jnp.concatenate([piece[:, :HALF], piece[:, HALF:]], axis=0).astype(BF16)
    send_x(4)

    own_dp.wait()
    for copy in sent_dp:
        copy.wait_recv()
    value = r_dp[0]
    for k in range(1, NDP):
        value = value + r_dp[k]
    vec_z[...] = value
    send_z(2)
    arrived_z(2)
    value = r_z[0]
    for k in range(1, NZ):
        value = value + r_z[k]
    vec_x[...] = value
    send_x(5)
    arrived_x(5)
    sums_out[...] = r_x[...]
    for k in range(5):
        arrived_x(k)

    @pl.when(z >= WIN - 1)
    def _():
        head.wait_send()

    for s in range(1, WIN - 1):

        @pl.when(z >= WIN - 1 - s)
        def _():
            ring[s - 1].wait_send()

    for group in sent + sent_z:
        for copy in group:
            copy.wait_send()
    for copy in sent_dp:
        copy.wait_send()


def by_head(a):
    lead = a.shape[:-1]
    parts = [
        a[..., : NX * QC].reshape(*lead, NX, QC),
        a[..., NX * QC : NX * (QC + HD)].reshape(*lead, NX, HD),
        a[..., NX * (QC + HD) :].reshape(*lead, NX, HD),
    ]
    return jnp.concatenate(parts, axis=-1)


def from_heads(a):
    lead = a.shape[:-2]
    parts = [a[..., :QC], a[..., QC : QC + HD], a[..., QC + HD :]]
    return jnp.concatenate([part.reshape(*lead, -1) for part in parts], axis=-1)


def shape(dims, kind):
    return jax.ShapeDtypeStruct(dims, kind)


ANY = pl.BlockSpec(memory_space=pl.ANY)
VMEM = pl.BlockSpec(memory_space=pltpu.VMEM)
DMA = pltpu.SemaphoreType.DMA
LIMIT = 56 * 1024 * 1024


def per_device(
    text_rows, image_rows, tile_counts, tile_offsets, doc_ids, out_grad, proj_scale, proj_shift
):
    image = by_head(image_rows[0]).reshape(SLOTS, NX, 2, HALF)
    image = image.transpose(1, 2, 0, 3).reshape(NX, 16, HALF)
    slot = jnp.arange(TOK, dtype=jnp.int32)
    target = jnp.where(slot < tile_counts[0, 0], tile_offsets[0, 0] + slot, -(1 << 20))
    meta = jnp.concatenate([doc_ids, target[None], jnp.zeros((6, TOK), jnp.int32)], axis=0)
    proj = jnp.concatenate([by_head(proj_scale), by_head(proj_shift)], axis=0)

    q, do, kvw, images, metas = pl.pallas_call(
        spread_kernel,
        out_shape=(
            shape((ROW, QC), BF16),
            shape((ROW, QC), BF16),
            shape((WIN, ROW, 2 * HD), BF16),
            shape((NZ * NX, 16, HALF), BF16),
            shape((NZ * NX, 8, TOK), jnp.int32),
        ),
        in_specs=[ANY] * 4,
        out_specs=(ANY,) * 5,
        scratch_shapes=[
            DMA((6,)), DMA((3, 6)), DMA((3, 6)), DMA((5,)), DMA((5,)),
            DMA((4, 2)), DMA((4, 2)), DMA((3, 2)), DMA((3, 2)),
        ],
        compiler_params=pltpu.CompilerParams(collective_id=0, has_side_effects=True),
        name="spread",
    )(text_rows[0], out_grad[0], image, meta)

    docs = metas[:, 0, :]
    targets = metas[:, 1, :SLOTS].reshape(NSLOT)

    attn, dqm, part, scatq, sums, onehot_t, keep, rawkv = pl.pallas_call(
        attend_kernel,
        out_shape=(
            shape((ROW, QC), BF16),
            shape((ROW, QC), BF16),
            shape((WIN, ROW, 2 * HD), BF16),
            shape((NSLOT, QC), BF16),
            shape((24, HD), F32),
            shape((NSLOT, ROW), BF16),
            shape((ROW, HD), F32),
            shape((NSLOT, 2 * HD), BF16),
        ),
        in_specs=[VMEM] * 8,
        out_specs=(VMEM,) * 8,
        scratch_shapes=[
            pltpu.VMEM((NSLOT, HC), BF16),
            pltpu.VMEM((NSLOT, HC), BF16),
            pltpu.VMEM((ROW, QC), BF16),
            pltpu.VMEM((ROW, QC), BF16),
            pltpu.VMEM((WIN, ROW, HD), BF16),
            pltpu.VMEM((WIN, ROW, HD), BF16),
            pltpu.VMEM((WIN, HD, ROW), BF16),
            pltpu.VMEM((WIN, HD, ROW), BF16),
            pltpu.VMEM((WIN, ROW, ROW), F32),
            pltpu.VMEM((WIN, ROW, ROW), BF16),
            pltpu.VMEM((HD, ROW), F32),
            pltpu.VMEM((WIN, ROW, 2 * HD), F32),
        ],
        compiler_params=pltpu.CompilerParams(vmem_limit_bytes=LIMIT),
        name="attend",
    )(q, do, kvw, images, docs, targets[None, :], targets[:, None], proj)

    attn_out, text_grad, image_out, sums = pl.pallas_call(
        return_kernel,
        out_shape=(
            shape((TOK, NX * QC), BF16),
            shape((TOK, NX * HC), BF16),
            shape((NX, 16, HALF), BF16),
            shape((NX, 24, HD), F32),
        ),
        in_specs=[ANY, ANY, VMEM, VMEM, VMEM, VMEM, VMEM, VMEM, VMEM],
        out_specs=(ANY, ANY, ANY, VMEM),
        scratch_shapes=[
            pltpu.VMEM((TOK, 2 * HD), BF16),
            pltpu.VMEM((4, ROW, 2 * HD), BF16),
            pltpu.VMEM((4, ROW, 2 * HD), BF16),
            pltpu.VMEM((ROW, 2 * HD), BF16),
            pltpu.VMEM((ROW, 2 * HD), BF16),
            pltpu.VMEM((NSLOT, 2 * HD), BF16),
            pltpu.VMEM((NZ, 32, QC), BF16),
            pltpu.VMEM((NZ, 32, 2 * HD), BF16),
            pltpu.VMEM((NX, 16, HALF), BF16),
            pltpu.VMEM((24, HD), F32),
            pltpu.VMEM((24, HD), F32),
            pltpu.VMEM((24, HD), F32),
            pltpu.VMEM((NDP, 24, HD), F32),
            pltpu.VMEM((NZ, 24, HD), F32),
            pltpu.VMEM((NX, 24, HD), F32),
            DMA((10,)), DMA((3, 6)), DMA((3, 6)), DMA((5,)), DMA((5,)),
            DMA((7, 3)), DMA((7, 3)), DMA((7,)), DMA((7,)),
        ],
        compiler_params=pltpu.CompilerParams(
            collective_id=1, has_side_effects=True, vmem_limit_bytes=LIMIT
        ),
        name="give_back",
    )(attn, dqm, part, scatq, sums, onehot_t, keep, rawkv, proj)

    image_grad = image_out.reshape(NX, 2, SLOTS, HALF).transpose(2, 0, 1, 3).reshape(SLOTS, NX, HC)
    image_grad = from_heads(image_grad)[None]
    scale_grad = from_heads(sums[:, :10].reshape(NX, HC))
    shift_grad = from_heads(sums[:, 10:20].reshape(NX, HC))
    return (attn_out[None], text_grad[None], image_grad, scale_grad, shift_grad)


def solution(mesh):
    return jax.shard_map(
        per_device,
        mesh=mesh,
        in_specs=(
            P("dp", "ctx", None),
            P("dp", "ctx", None),
            P("dp", "ctx"),
            P("dp", "ctx"),
            P("dp", "ctx"),
            P("dp", "ctx", None),
            P(),
            P(),
        ),
        out_specs=(P("dp", "ctx", None), P("dp", "ctx", None), P("dp", "ctx", None), P(), P()),
        check_vma=False,
    )
```

```python
import math

import jax
import jax.numpy as jnp
from jax import lax
from jax.experimental import pallas as pl
from jax.experimental.pallas import tpu as pltpu
from jax.sharding import PartitionSpec as P

MESH = pl.DeviceIdType.MESH
HD = 128
REP = 8
DOCS = 8
NZ = 8
NX = 4
NDP = 8
TOK = 128
ROW = NX * TOK
SLOTS = 8
NSLOT = NZ * NX * SLOTS
QC = REP * HD
HC = QC + 2 * HD
WIN = 6
HALF = HC // 2
LANES = REP * TOK
SCALE = HD ** -0.5
LOG2E = math.log2(math.e)
F32 = jnp.float32
BF16 = jnp.bfloat16


def place():
    ctx = lax.axis_index("ctx")
    return lax.axis_index("dp"), ctx // NX, ctx % NX


def ctx_of(z, x):
    return {"ctx": z * NX + x}


def remote(src, dst, send, recv, device):
    return pltpu.make_async_remote_copy(
        src_ref=src, dst_ref=dst, send_sem=send, recv_sem=recv, device_id=device, device_id_type=MESH
    )


def cols(start, size):
    return pl.ds(pl.multiple_of(start, HD), size)


def rows_of(start, size):
    return pl.ds(pl.multiple_of(start, size), size)


def greet(devices):
    barrier = pltpu.get_barrier_semaphore()
    for device in devices:
        pl.semaphore_signal(barrier, inc=1, device_id=device, device_id_type=MESH)
    pl.semaphore_wait(barrier, len(devices))


def layer_kernel(
    text, dout, image, meta, proj,
    attn_out, text_grad, image_out, sums_out,
    q_in, do_in, kvw, images, metas, raw, adapted, onehot_t, keep, starts,
    q_t, do_t, q_s, do_s, ks, vs, kts, vts, p_buf, p_first, acc_t, top, total, tops, corr, dkv,
    attn, dq, first_in, first_out, ring_in, ring_out, whole, mkv, scatq, scatkv, rxq, rxkv, igs,
    vec, vec_z, vec_x, r_dp, r_z, r_x,
    own_sem, x_send, x_recv, kv_send, kv_recv, up_send, up_recv, down_send, down_recv,
    ring_send, ring_recv, z_send, z_recv, dp_send, dp_recv,
):
    dp, z, x = place()
    up, down = (z + 1) % NZ, (z + NZ - 1) % NZ
    me = z * NX + x
    base = z * ROW
    greet(
        [ctx_of(z, (x + d) % NX) for d in range(1, NX)]
        + [ctx_of((z + d) % NZ, x) for d in range(1, NZ)]
        + [{"dp": (dp + d) % NDP} for d in range(1, NDP)]
    )

    def pieces(peer):
        own_rows = rows_of(x * TOK, TOK)
        return [
            (meta, metas.at[me]),
            (image.at[peer], images.at[me]),
            (text.at[:, cols(NX * QC + peer * HD, HD)], kvw.at[WIN - 1, own_rows, pl.ds(0, HD)]),
            (text.at[:, cols(NX * QC + (NX + peer) * HD, HD)], kvw.at[WIN - 1, own_rows, pl.ds(HD, HD)]),
            (text.at[:, cols(peer * QC, QC)], q_in.at[x]),
            (dout.at[:, cols(peer * QC, QC)], do_in.at[x]),
            (attn.at[peer], attn_out.at[:, cols(x * QC, QC)]),
            (dq.at[peer], text_grad.at[:, cols(x * QC, QC)]),
            (mkv.at[rows_of(peer * TOK, TOK), pl.ds(0, HD)], text_grad.at[:, cols(NX * QC + x * HD, HD)]),
            (mkv.at[rows_of(peer * TOK, TOK), pl.ds(HD, HD)], text_grad.at[:, cols(NX * QC + (NX + x) * HD, HD)]),
            (igs.at[peer], image_out.at[x]),
            (vec_x, r_x.at[x]),
        ]

    own_x = [pltpu.make_async_copy(src, dst, own_sem.at[k]) for k, (src, dst) in enumerate(pieces(x))]
    sent_x = []
    for d in range(1, NX):
        peer = (x + d) % NX
        sent_x.append([
            remote(src, dst, x_send.at[d - 1, k], x_recv.at[d - 1, k], ctx_of(z, peer))
            for k, (src, dst) in enumerate(pieces(peer))
        ])

    def send_x(k):
        for d in range(NX - 1):
            sent_x[d][k].start()
        own_x[k].start()

    def arrived_x(k):
        own_x[k].wait()
        for d in range(NX - 1):
            sent_x[d][k].wait_recv()

    for k in range(6):
        send_x(k)

    ups, downs = [], []
    for k in range(3):
        block = pl.ds(((z + NZ - k) % NZ) * NX, NX)
        ups.append([
            remote(a.at[block], a.at[block], up_send.at[k, j], up_recv.at[k, j], ctx_of(up, x))
            for j, a in enumerate((metas, images))
        ])
    for k in range(4):
        block = pl.ds(((z + k) % NZ) * NX, NX)
        downs.append([
            remote(a.at[block], a.at[block], down_send.at[k, j], down_recv.at[k, j], ctx_of(down, x))
            for j, a in enumerate((metas, images))
        ])

    def passed(k):
        return remote(
            kvw.at[WIN - 1 - k], kvw.at[WIN - 2 - k], kv_send.at[k], kv_recv.at[k], ctx_of(up, x)
        )

    tail = pl.ds(ROW - TOK, TOK)
    last = remote(kvw.at[1, tail], kvw.at[0, tail], kv_send.at[4], kv_recv.at[4], ctx_of(up, x))

    arrived_x(0)
    arrived_x(1)
    for j in range(2):
        ups[0][j].start()
        downs[0][j].start()
    arrived_x(2)
    arrived_x(3)

    @pl.when(z <= NZ - 2)
    def _():
        passed(0).start()

    for k in range(1, 5):
        for j in range(2):
            if k <= 3:
                ups[k - 1][j].wait_recv()
            if k < 3:
                ups[k][j].start()
            downs[k - 1][j].wait_recv()
            if k < 4:
                downs[k][j].start()

    scale = proj[pl.ds(x, 1), :]
    shift = proj[pl.ds(NX + x, 1), :]

    def adapt(pair, _):
        first = images[2 * pair].astype(F32)
        second = images[2 * pair + 1].astype(F32)
        left = jnp.concatenate([first[:8], second[:8]], axis=0)
        right = jnp.concatenate([first[8:], second[8:]], axis=0)
        at = rows_of(pair * 16, 16)
        raw[at, pl.ds(0, HALF)] = left.astype(BF16)
        raw[at, pl.ds(HALF, HALF)] = right.astype(BF16)
        adapted[at, pl.ds(0, HALF)] = (left * scale[:, :HALF] + shift[:, :HALF]).astype(BF16)
        adapted[at, pl.ds(HALF, HALF)] = (right * scale[:, HALF:] + shift[:, HALF:]).astype(BF16)
        return 0

    lax.fori_loop(0, NSLOT // 16, adapt, 0)
    all_metas = jnp.sum(metas[:, 1:3, :], axis=0)
    target = jnp.concatenate([all_metas[0:1], all_metas[1:2]], axis=1) - 1
    all_docs = metas[:, 0, :]
    before = [
        jnp.sum(jnp.where(all_docs < doc, 1, 0).astype(F32), axis=(0, 1), keepdims=True).astype(jnp.int32)
        for doc in range(1, DOCS)
    ]

    def chosen(begin, size):
        position = begin + lax.broadcasted_iota(jnp.int32, (size, NSLOT), 0)
        hit = jnp.where(position == target, 1.0, 0.0).astype(F32)
        return hit, jnp.max(hit, axis=1, keepdims=True)

    arrived_x(4)

    def place_queries(a, _):
        hit, is_image = chosen(base + a * TOK, TOK)
        onehot_t[:, cols(a * TOK, TOK)] = hit.T.astype(BF16)
        keep[rows_of(a * TOK, TOK), :] = jnp.broadcast_to(1.0 - is_image, (TOK, HD))
        picked = jnp.dot(hit.astype(BF16), adapted[:, :QC], preferred_element_type=F32)
        value = jnp.where(is_image > 0.0, picked, q_in[a].astype(F32))
        for r in range(REP):
            piece = value[:, r * HD : (r + 1) * HD]
            q_s[a, r * HD : (r + 1) * HD, :] = piece.astype(BF16)
            q_t[a, :, r * HD : (r + 1) * HD] = piece.T.astype(BF16)
        docs = metas[z * NX + a, 0:1, :]
        start = jnp.zeros((1, TOK), jnp.int32)
        for doc in range(1, DOCS):
            start = jnp.where(docs == doc, before[doc - 1], start)
        starts[a] = jnp.concatenate([start] * REP, axis=1)
        top[a] = jnp.full((1, LANES), -1e30, F32)
        total[a] = jnp.zeros((1, LANES), F32)
        acc_t[a] = jnp.zeros((HD, LANES), F32)
        return 0

    lax.fori_loop(0, NX, place_queries, 0)

    def place_keys(s, at, size):
        hit, is_image = chosen(base + (s - (WIN - 1)) * ROW + at, size)
        picked = jnp.dot(hit.astype(BF16), adapted[:, QC:], preferred_element_type=F32)
        both = jnp.where(is_image > 0.0, picked, kvw[s, at : at + size].astype(F32))
        ks[s, at : at + size, :] = both[:, :HD].astype(BF16)
        vs[s, at : at + size, :] = both[:, HD:].astype(BF16)
        kts[s, :, at : at + size] = both[:, :HD].T.astype(BF16)
        vts[s, :, at : at + size] = both[:, HD:].T.astype(BF16)

    within = lax.broadcasted_iota(jnp.int32, (1, TOK), 1)
    within = jnp.concatenate([within] * REP, axis=1)

    def forward(s, a, at, size, keep_prob):
        key_pos = base + (s - (WIN - 1)) * ROW + at + lax.broadcasted_iota(jnp.int32, (size, 1), 0)
        value = jnp.dot(ks[s, at : at + size, :], q_t[a], preferred_element_type=F32) * (SCALE * LOG2E)
        value = jnp.where((key_pos >= starts[a]) & (key_pos <= base + a * TOK + within), value, -1e30)
        old = top[a]
        new = jnp.maximum(old, jnp.max(value, axis=0, keepdims=True))
        top[a] = new
        tops[s, a] = new
        factor = jnp.exp2(old - new)
        prob = jnp.exp2(value - new)
        total[a] = total[a] * factor + jnp.sum(prob, axis=0, keepdims=True)
        prob_b = prob.astype(BF16)
        keep_prob(prob_b)
        acc_t[a] = acc_t[a] * factor + jnp.dot(vts[s, :, at : at + size], prob_b, preferred_element_type=F32)

    def forward_row(k, _):
        s = WIN - 1 - k

        @pl.when(k >= 1)
        def _():
            passed(k - 1).wait_recv()

        @pl.when((k >= 1) & (k <= 3) & (z <= NZ - 2))
        def _():
            passed(k).start()

        @pl.when((k == 4) & (z <= NZ - 2))
        def _():
            last.start()

        place_keys(s, 0, ROW)

        def one(a, _):
            def keep_prob(prob):
                p_buf[s - 1, a] = prob

            forward(s, a, 0, ROW, keep_prob)
            return 0

        lax.fori_loop(0, NX, one, 0)
        return 0

    lax.fori_loop(0, jnp.minimum(z + 1, 5), forward_row, 0)

    @pl.when(z >= WIN - 1)
    def _():
        last.wait_recv()
        place_keys(0, ROW - TOK, TOK)

        def keep_prob(prob):
            p_first[...] = prob

        forward(0, 0, ROW - TOK, TOK, keep_prob)

    arrived_x(5)

    def finish(a, _):
        for r in range(REP):
            piece = do_in[a, :, r * HD : (r + 1) * HD]
            do_s[a, r * HD : (r + 1) * HD, :] = piece
            do_t[a, :, r * HD : (r + 1) * HD] = piece.astype(F32).T.astype(BF16)
        inverse = 1.0 / total[a]
        total[a] = inverse
        out_t = (acc_t[a] * inverse).astype(BF16).astype(F32)
        corr[a] = jnp.sum(do_t[a].astype(F32) * out_t, axis=0, keepdims=True)
        for r in range(REP):
            attn[a, :, r * HD : (r + 1) * HD] = out_t[:, r * HD : (r + 1) * HD].T.astype(BF16)
        acc_t[a] = jnp.zeros((HD, LANES), F32)
        return 0

    lax.fori_loop(0, NX, finish, 0)
    send_x(6)

    def backward(s, a, at, size, prob_b):
        part = jnp.exp2(tops[s, a] - top[a]) * total[a]
        prob = prob_b.astype(F32) * part
        dprob = jnp.dot(vs[s, at : at + size, :], do_t[a], preferred_element_type=F32)
        dscore = (prob * (dprob - corr[a])).astype(BF16)
        acc_t[a] += jnp.dot(kts[s, :, at : at + size], dscore, preferred_element_type=F32)
        dk = jnp.dot(dscore, q_s[a], preferred_element_type=F32)
        dv = jnp.dot(prob.astype(BF16), do_s[a], preferred_element_type=F32)
        return dk, dv

    first = remote(first_out, first_in, ring_send.at[0], ring_recv.at[0], ctx_of(down, x))
    ring = [
        remote(ring_out.at[k], ring_in.at[k], ring_send.at[1 + k], ring_recv.at[1 + k], ctx_of(down, x))
        for k in range(4)
    ]

    @pl.when(z >= WIN - 1)
    def _():
        dk, dv = backward(0, 0, ROW - TOK, TOK, p_first[...])
        first_out[:, :HD] = (dk * SCALE).astype(BF16)
        first_out[:, HD:] = dv.astype(BF16)
        first.start()

    def backward_row(s):
        def one(a, _):
            dk, dv = backward(s, a, 0, ROW, p_buf[s - 1, a])

            @pl.when(a == 0)
            def _():
                dkv[:, :HD] = dk
                dkv[:, HD:] = dv

            @pl.when(a > 0)
            def _():
                dkv[:, :HD] += dk
                dkv[:, HD:] += dv

            return 0

        lax.fori_loop(0, NX, one, 0)
        dkv[:, :HD] = dkv[:, :HD] * SCALE

    def add_arrived(s):
        @pl.when(z <= NZ - 2)
        def _():
            if s == 1:
                first.wait_recv()
                dkv[ROW - TOK :, :] += first_in[...].astype(F32)
            else:
                ring[s - 2].wait_recv()
                dkv[...] += ring_in[s - 2].astype(F32)

    for s in range(1, WIN - 1):

        @pl.when(z >= WIN - 1 - s)
        def _():
            backward_row(s)
            add_arrived(s)
            ring_out[s - 1] = dkv[...].astype(BF16)
            ring[s - 1].start()

    backward_row(WIN - 1)

    def give(a, _):
        kept = keep[rows_of(a * TOK, TOK), :]
        value = acc_t[a] * SCALE
        for r in range(REP):
            piece = value[:, r * HD : (r + 1) * HD].T.astype(BF16)
            q_s[a, r * HD : (r + 1) * HD, :] = piece
            dq[a, :, r * HD : (r + 1) * HD] = (piece.astype(F32) * kept).astype(BF16)
        return 0

    lax.fori_loop(0, NX, give, 0)
    send_x(7)

    def z_pieces(peer):
        return [
            (scatq.at[rows_of(peer * 32, 32)], rxq.at[z]),
            (scatkv.at[rows_of(peer * 32, 32)], rxkv.at[z]),
            (vec_z, r_z.at[z]),
        ]

    own_z = [pltpu.make_async_copy(src, dst, own_sem.at[12 + k]) for k, (src, dst) in enumerate(z_pieces(z))]
    sent_z = []
    for d in range(1, NZ):
        peer = (z + d) % NZ
        sent_z.append([
            remote(src, dst, z_send.at[d - 1, k], z_recv.at[d - 1, k], ctx_of(peer, x))
            for k, (src, dst) in enumerate(z_pieces(peer))
        ])

    def send_z(k):
        for d in range(NZ - 1):
            sent_z[d][k].start()
        own_z[k].start()

    def arrived_z(k):
        own_z[k].wait()
        for d in range(NZ - 1):
            sent_z[d][k].wait_recv()

    vec[...] = jnp.zeros_like(vec)
    for r in range(REP):
        at = slice(r * HD, (r + 1) * HD)
        grads = jnp.concatenate([q_s[a, at, :] for a in range(NX)], axis=0)
        scattered = jnp.dot(onehot_t[...], grads, preferred_element_type=F32)
        scatq[:, at] = scattered.astype(BF16)
        vec[r : r + 1, :] = jnp.sum(scattered * raw[:, at].astype(F32), axis=0, keepdims=True)
        vec[10 + r : 11 + r, :] = jnp.sum(scattered, axis=0, keepdims=True)
    send_z(0)

    add_arrived(WIN - 1)
    whole[...] = dkv[...].astype(BF16)
    for k in range(2):
        at = slice(k * HD, (k + 1) * HD)
        mkv[:, at] = (whole[:, at].astype(F32) * keep[...]).astype(BF16)
    send_x(8)
    send_x(9)
    scattered = jnp.dot(onehot_t[...], whole[...], preferred_element_type=F32)
    scatkv[...] = scattered.astype(BF16)
    send_z(1)
    scale_part = jnp.sum(scattered * raw[:, QC:].astype(F32), axis=0, keepdims=True)
    shift_part = jnp.sum(scattered, axis=0, keepdims=True)
    for k in range(2):
        vec[REP + k : REP + k + 1, :] = scale_part[:, k * HD : (k + 1) * HD]
        vec[10 + REP + k : 11 + REP + k, :] = shift_part[:, k * HD : (k + 1) * HD]
    own_dp = pltpu.make_async_copy(vec, r_dp.at[dp], own_sem.at[15])
    sent_dp = [
        remote(vec, r_dp.at[dp], dp_send.at[d - 1], dp_recv.at[d - 1], {"dp": (dp + d) % NDP}) for d in range(1, NDP)
    ]
    for copy in sent_dp:
        copy.start()
    own_dp.start()

    own_dp.wait()
    for copy in sent_dp:
        copy.wait_recv()
    value = r_dp[0]
    for k in range(1, NDP):
        value = value + r_dp[k]
    vec_z[...] = value
    send_z(2)

    arrived_z(0)
    arrived_z(1)
    slots_q = rxq[0].astype(F32)
    slots_kv = rxkv[0].astype(F32)
    for k in range(1, NZ):
        slots_q = slots_q + rxq[k].astype(F32)
        slots_kv = slots_kv + rxkv[k].astype(F32)
    grad = jnp.concatenate([slots_q, slots_kv], axis=1) * proj[pl.ds(x, 1), :]
    for k in range(NX):
        piece = grad[k * SLOTS : (k + 1) * SLOTS]
        igs[k] = jnp.concatenate([piece[:, :HALF], piece[:, HALF:]], axis=0).astype(BF16)
    send_x(10)

    arrived_z(2)
    value = r_z[0]
    for k in range(1, NZ):
        value = value + r_z[k]
    vec_x[...] = value
    send_x(11)
    arrived_x(11)
    sums_out[...] = r_x[...]
    for k in range(6, 11):
        arrived_x(k)

    for k in range(4):

        @pl.when((z >= k) & (z <= NZ - 2))
        def _():
            passed(k).wait_send()

        @pl.when(z >= k + 1)
        def _():
            ring[3 - k].wait_send()

    @pl.when((z >= 4) & (z <= NZ - 2))
    def _():
        last.wait_send()

    @pl.when(z >= WIN - 1)
    def _():
        first.wait_send()

    for group in sent_x + sent_z + ups + downs:
        for copy in group:
            copy.wait_send()
    for copy in sent_dp:
        copy.wait_send()


def by_head(a):
    lead = a.shape[:-1]
    parts = [
        a[..., : NX * QC].reshape(*lead, NX, QC),
        a[..., NX * QC : NX * (QC + HD)].reshape(*lead, NX, HD),
        a[..., NX * (QC + HD) :].reshape(*lead, NX, HD),
    ]
    return jnp.concatenate(parts, axis=-1)


def from_heads(a):
    lead = a.shape[:-2]
    parts = [a[..., :QC], a[..., QC : QC + HD], a[..., QC + HD :]]
    return jnp.concatenate([part.reshape(*lead, -1) for part in parts], axis=-1)


def shape(dims, kind):
    return jax.ShapeDtypeStruct(dims, kind)


ANY = pl.BlockSpec(memory_space=pl.ANY)
VMEM = pl.BlockSpec(memory_space=pltpu.VMEM)
DMA = pltpu.SemaphoreType.DMA
LIMIT = 60 * 1024 * 1024


def per_device(
    text_rows, image_rows, tile_counts, tile_offsets, doc_ids, out_grad, proj_scale, proj_shift
):
    image = by_head(image_rows[0]).reshape(SLOTS, NX, 2, HALF)
    image = image.transpose(1, 2, 0, 3).reshape(NX, 16, HALF)
    slot = jnp.arange(TOK, dtype=jnp.int32)
    me = lax.axis_index("ctx")
    within = slot - SLOTS * (me % 16)
    live = (within >= 0) & (within < tile_counts[0, 0])
    target = jnp.where(live, tile_offsets[0, 0] + within + 1, 0)[None]
    row = jnp.arange(8, dtype=jnp.int32)[:, None]
    meta = jnp.where(row == 0, doc_ids, jnp.where(row == 1 + me // 16, target, 0))
    proj = jnp.concatenate([by_head(proj_scale), by_head(proj_shift)], axis=0)

    attn_out, text_grad, image_out, sums = pl.pallas_call(
        layer_kernel,
        out_shape=(
            shape((TOK, NX * QC), BF16),
            shape((TOK, NX * HC), BF16),
            shape((NX, 16, HALF), BF16),
            shape((NX, 24, HD), F32),
        ),
        in_specs=[ANY, ANY, ANY, ANY, VMEM],
        out_specs=(ANY, ANY, ANY, VMEM),
        scratch_shapes=[
            pltpu.VMEM((NX, TOK, QC), BF16),
            pltpu.VMEM((NX, TOK, QC), BF16),
            pltpu.VMEM((WIN, ROW, 2 * HD), BF16),
            pltpu.VMEM((NZ * NX, 16, HALF), BF16),
            pltpu.VMEM((NZ * NX, 8, TOK), jnp.int32),
            pltpu.VMEM((NSLOT, HC), BF16),
            pltpu.VMEM((NSLOT, HC), BF16),
            pltpu.VMEM((NSLOT, ROW), BF16),
            pltpu.VMEM((ROW, HD), F32),
            pltpu.VMEM((NX, 1, LANES), jnp.int32),
            pltpu.VMEM((NX, HD, LANES), BF16),
            pltpu.VMEM((NX, HD, LANES), BF16),
            pltpu.VMEM((NX, LANES, HD), BF16),
            pltpu.VMEM((NX, LANES, HD), BF16),
            pltpu.VMEM((WIN, ROW, HD), BF16),
            pltpu.VMEM((WIN, ROW, HD), BF16),
            pltpu.VMEM((WIN, HD, ROW), BF16),
            pltpu.VMEM((WIN, HD, ROW), BF16),
            pltpu.VMEM((WIN - 1, NX, ROW, LANES), BF16),
            pltpu.VMEM((TOK, LANES), BF16),
            pltpu.VMEM((NX, HD, LANES), F32),
            pltpu.VMEM((NX, 1, LANES), F32),
            pltpu.VMEM((NX, 1, LANES), F32),
            pltpu.VMEM((WIN, NX, 1, LANES), F32),
            pltpu.VMEM((NX, 1, LANES), F32),
            pltpu.VMEM((ROW, 2 * HD), F32),
            pltpu.VMEM((NX, TOK, QC), BF16),
            pltpu.VMEM((NX, TOK, QC), BF16),
            pltpu.VMEM((TOK, 2 * HD), BF16),
            pltpu.VMEM((TOK, 2 * HD), BF16),
            pltpu.VMEM((4, ROW, 2 * HD), BF16),
            pltpu.VMEM((4, ROW, 2 * HD), BF16),
            pltpu.VMEM((ROW, 2 * HD), BF16),
            pltpu.VMEM((ROW, 2 * HD), BF16),
            pltpu.VMEM((NSLOT, QC), BF16),
            pltpu.VMEM((NSLOT, 2 * HD), BF16),
            pltpu.VMEM((NZ, 32, QC), BF16),
            pltpu.VMEM((NZ, 32, 2 * HD), BF16),
            pltpu.VMEM((NX, 16, HALF), BF16),
            pltpu.VMEM((24, HD), F32),
            pltpu.VMEM((24, HD), F32),
            pltpu.VMEM((24, HD), F32),
            pltpu.VMEM((NDP, 24, HD), F32),
            pltpu.VMEM((NZ, 24, HD), F32),
            pltpu.VMEM((NX, 24, HD), F32),
            DMA((16,)), DMA((3, 12)), DMA((3, 12)), DMA((5,)), DMA((5,)),
            DMA((3, 2)), DMA((3, 2)), DMA((4, 2)), DMA((4, 2)),
            DMA((5,)), DMA((5,)), DMA((7, 3)), DMA((7, 3)), DMA((7,)), DMA((7,)),
        ],
        compiler_params=pltpu.CompilerParams(
            collective_id=0, has_side_effects=True, vmem_limit_bytes=LIMIT
        ),
        name="layer",
    )(text_rows[0], out_grad[0], image, meta, proj)

    image_grad = image_out.reshape(NX, 2, SLOTS, HALF).transpose(2, 0, 1, 3).reshape(SLOTS, NX, HC)
    image_grad = from_heads(image_grad)[None]
    scale_grad = from_heads(sums[:, :10].reshape(NX, HC))
    shift_grad = from_heads(sums[:, 10:20].reshape(NX, HC))
    return (attn_out[None], text_grad[None], image_grad, scale_grad, shift_grad)


def solution(mesh):
    return jax.shard_map(
        per_device,
        mesh=mesh,
        in_specs=(
            P("dp", "ctx", None),
            P("dp", "ctx", None),
            P("dp", "ctx"),
            P("dp", "ctx"),
            P("dp", "ctx"),
            P("dp", "ctx", None),
            P(),
            P(),
        ),
        out_specs=(P("dp", "ctx", None), P("dp", "ctx", None), P("dp", "ctx", None), P(), P()),
        check_vma=False,
    )
```

```python
import math

import jax
import jax.numpy as jnp
from jax import lax
from jax.experimental import pallas as pl
from jax.experimental.pallas import tpu as pltpu
from jax.sharding import PartitionSpec as P

MESH = pl.DeviceIdType.MESH
HD = 128
REP = 8
DOCS = 8
NZ = 8
NX = 4
NDP = 8
TOK = 128
ROW = NX * TOK
SLOTS = 8
NSLOT = NZ * NX * SLOTS
QC = REP * HD
HC = QC + 2 * HD
WIN = 6
HALF = HC // 2
LANES = REP * TOK
SCALE = HD ** -0.5
LOG2E = math.log2(math.e)
F32 = jnp.float32
BF16 = jnp.bfloat16


def place():
    ctx = lax.axis_index("ctx")
    return lax.axis_index("dp"), ctx // NX, ctx % NX


def ctx_of(z, x):
    return {"ctx": z * NX + x}


def remote(src, dst, send, recv, device):
    return pltpu.make_async_remote_copy(
        src_ref=src, dst_ref=dst, send_sem=send, recv_sem=recv, device_id=device, device_id_type=MESH
    )


def cols(start, size):
    return pl.ds(pl.multiple_of(start, HD), size)


def rows_of(start, size):
    return pl.ds(pl.multiple_of(start, size), size)


def greet(devices):
    barrier = pltpu.get_barrier_semaphore()
    for device in devices:
        pl.semaphore_signal(barrier, inc=1, device_id=device, device_id_type=MESH)
    pl.semaphore_wait(barrier, len(devices))


def layer_kernel(
    text, dout, image_rows, counts, offsets, doc_ids, proj_scale, proj_shift,
    attn_out, text_grad, image_grad, scale_out, shift_out,
    image, meta, image_out, q_in, do_in, kvw, images, metas, raw, adapted, onehot_t, keep,
    q_t, do_t, q_s, do_s, ks, vs, kts, vts, p_buf, p_first, acc_t, top, total, tops, corr, dkv,
    attn, dq, first_in, first_out, ring_in, ring_out, whole, mkv, scatq, scatkv, rxq, rxkv, igs,
    vec, vec_z, vec_x, r_dp, r_z, r_x,
    img_send, img_recv, key_send, key_recv, own_sem, x_send, x_recv, kv_send, kv_recv, up_send, up_recv, down_send, down_recv,
    ring_send, ring_recv, z_send, z_recv, dp_send, dp_recv,
):
    dp, z, x = place()
    up, down = (z + 1) % NZ, (z + NZ - 1) % NZ
    me = z * NX + x
    base = z * ROW

    def of_head(ref, head):
        parts = [ref[pl.ds(head * REP + r, 1), :] for r in range(REP)]
        parts += [ref[pl.ds(NX * REP + head, 1), :], ref[pl.ds(NX * (REP + 1) + head, 1), :]]
        return jnp.concatenate(parts, axis=1)

    for head in range(NX):
        key, val = NX * QC + head * HD, NX * (QC + HD) + head * HD
        both = jnp.concatenate(
            [image_rows[:, head * QC : (head + 1) * QC], image_rows[:, key : key + HD], image_rows[:, val : val + HD]],
            axis=1,
        ).astype(F32)
        image[head] = jnp.concatenate([both[:, :HALF], both[:, HALF:]], axis=0).astype(BF16)
    lane = lax.broadcasted_iota(jnp.int32, (8, TOK), 1) - SLOTS * (me % 16)
    row = lax.broadcasted_iota(jnp.int32, (8, TOK), 0)
    live = (lane >= 0) & (lane < counts[...])
    filled = jnp.where(live, offsets[...] + lane + 1, 0)
    meta[...] = jnp.where(row == 0, doc_ids[...], jnp.where(row == 1 + me // 16, filled, 0))
    greet(
        [ctx_of(z, (x + d) % NX) for d in range(1, NX)]
        + [ctx_of((z + d) % NZ, x) for d in range(1, NZ)]
        + [{"dp": (dp + d) % NDP} for d in range(1, NDP)]
        + [ctx_of(near, (x + d) % NX) for near in (up, down) for d in range(1, NX)]
    )

    def pieces(peer):
        own_rows = rows_of(x * TOK, TOK)
        return [
            (meta, metas.at[me]),
            (image.at[peer], images.at[me]),
            (text.at[:, cols(NX * QC + peer * HD, HD)], kvw.at[WIN - 1, own_rows, pl.ds(0, HD)]),
            (text.at[:, cols(NX * QC + (NX + peer) * HD, HD)], kvw.at[WIN - 1, own_rows, pl.ds(HD, HD)]),
            (text.at[:, cols(peer * QC, QC)], q_in.at[x]),
            (dout.at[:, cols(peer * QC, QC)], do_in.at[x]),
            (attn.at[peer], attn_out.at[:, cols(x * QC, QC)]),
            (dq.at[peer], text_grad.at[:, cols(x * QC, QC)]),
            (mkv.at[rows_of(peer * TOK, TOK), pl.ds(0, HD)], text_grad.at[:, cols(NX * QC + x * HD, HD)]),
            (mkv.at[rows_of(peer * TOK, TOK), pl.ds(HD, HD)], text_grad.at[:, cols(NX * QC + (NX + x) * HD, HD)]),
            (igs.at[peer], image_out.at[x]),
            (vec_x, r_x.at[x]),
        ]

    own_x = [pltpu.make_async_copy(src, dst, own_sem.at[k]) for k, (src, dst) in enumerate(pieces(x))]
    sent_x = []
    for d in range(1, NX):
        peer = (x + d) % NX
        sent_x.append([
            remote(src, dst, x_send.at[d - 1, k], x_recv.at[d - 1, k], ctx_of(z, peer))
            for k, (src, dst) in enumerate(pieces(peer))
        ])

    def send_x(k):
        for d in range(NX - 1):
            sent_x[d][k].start()
        own_x[k].start()

    def arrived_x(k):
        own_x[k].wait()
        for d in range(NX - 1):
            sent_x[d][k].wait_recv()

    def image_step(near, way, d, k):
        head = (x + d) % NX
        src, dst = pieces(head)[k]
        return remote(src, dst, img_send.at[way, d, k], img_recv.at[way, x, k], ctx_of(near, head))

    def image_came(near, way, j, k):
        src, dst = pieces(j)[k]
        return remote(src, dst, img_send.at[way, 0, k], img_recv.at[way, j, k], ctx_of(near, j))

    def key_step(d, k):
        head = (x + d) % NX
        at = kvw.at[WIN - 2, rows_of(x * TOK, TOK), pl.ds(k * HD, HD)]
        src = text.at[:, cols(NX * QC + (NX * k + head) * HD, HD)]
        return remote(src, at, key_send.at[d, k], key_recv.at[x, k], ctx_of(up, head))

    def key_came(j, k):
        at = kvw.at[WIN - 2, rows_of(j * TOK, TOK), pl.ds(k * HD, HD)]
        src = text.at[:, cols(NX * QC + NX * k * HD, HD)]
        return remote(src, at, key_send.at[0, k], key_recv.at[j, k], ctx_of(up, x))

    send_x(0)
    send_x(1)
    for k in range(2):
        for d in range(NX):
            image_step(up, 0, d, k).start()
            image_step(down, 1, d, k).start()
    send_x(2)
    send_x(3)

    @pl.when(z <= NZ - 2)
    def _():
        for d in range(NX):
            for k in range(2):
                key_step(d, k).start()

    send_x(4)
    send_x(5)

    ups, downs = [None], [None]
    for k in range(1, 3):
        block = pl.ds(((z + NZ - k) % NZ) * NX, NX)
        ups.append([
            remote(a.at[block], a.at[block], up_send.at[k, j], up_recv.at[k, j], ctx_of(up, x))
            for j, a in enumerate((metas, images))
        ])
    for k in range(1, 4):
        block = pl.ds(((z + k) % NZ) * NX, NX)
        downs.append([
            remote(a.at[block], a.at[block], down_send.at[k, j], down_recv.at[k, j], ctx_of(down, x))
            for j, a in enumerate((metas, images))
        ])

    def hop(k, j):
        part = rows_of(j * TOK, TOK)
        return remote(
            kvw.at[WIN - 1 - k, part], kvw.at[WIN - 2 - k, part], kv_send.at[k, j], kv_recv.at[k, j], ctx_of(up, x)
        )

    def pass_keys(k, j):
        @pl.when(z >= k)
        def _():
            if k == 1:
                key_came(j, 0).wait_recv()
                key_came(j, 1).wait_recv()
            else:
                hop(k - 1, j).wait_recv()

        @pl.when((z >= k) & (z <= NZ - 2) & ((k < 4) | (j == NX - 1)))
        def _():
            hop(k, j).start()

    def pass_images(k):
        for j in range(2):
            if k == 1:
                for d in range(NX):
                    image_came(up, 0, d, j).wait_recv()
            elif k <= 3:
                ups[k - 1][j].wait_recv()
            if k < 3:
                ups[k][j].start()
            if k == 1:
                for d in range(NX):
                    image_came(down, 1, d, j).wait_recv()
            else:
                downs[k - 1][j].wait_recv()
            if k < 4:
                downs[k][j].start()

    pass_images(1)
    for j in range(NX):
        pass_keys(1, j)
    pass_images(2)
    for j in range(NX):
        pass_keys(2, j)
    pass_images(3)
    for k in range(4):
        arrived_x(k)
    pass_images(4)

    scale = of_head(proj_scale, x)
    shift = of_head(proj_shift, x)

    def adapt(pair, _):
        first = images[2 * pair].astype(F32)
        second = images[2 * pair + 1].astype(F32)
        left = jnp.concatenate([first[:8], second[:8]], axis=0)
        right = jnp.concatenate([first[8:], second[8:]], axis=0)
        at = rows_of(pair * 16, 16)
        raw[at, pl.ds(0, HALF)] = left.astype(BF16)
        raw[at, pl.ds(HALF, HALF)] = right.astype(BF16)
        adapted[at, pl.ds(0, HALF)] = (left * scale[:, :HALF] + shift[:, :HALF]).astype(BF16)
        adapted[at, pl.ds(HALF, HALF)] = (right * scale[:, HALF:] + shift[:, HALF:]).astype(BF16)
        return 0

    lax.fori_loop(0, NSLOT // 16, adapt, 0)
    all_metas = jnp.sum(metas[:, 1:3, :], axis=0)
    target = jnp.concatenate([all_metas[0:1], all_metas[1:2]], axis=1) - 1
    def chosen(begin, size):
        position = begin + lax.broadcasted_iota(jnp.int32, (size, NSLOT), 0)
        hit = jnp.where(position == target, 1.0, 0.0).astype(F32)
        return hit, jnp.max(hit, axis=1, keepdims=True)

    arrived_x(4)

    def place_queries(a, _):
        hit, is_image = chosen(base + a * TOK, TOK)
        onehot_t[:, cols(a * TOK, TOK)] = hit.T.astype(BF16)
        keep[rows_of(a * TOK, TOK), :] = jnp.broadcast_to(1.0 - is_image, (TOK, HD))
        picked = jnp.dot(hit.astype(BF16), adapted[:, :QC], preferred_element_type=F32)
        value = jnp.where(is_image > 0.0, picked, q_in[a].astype(F32))
        for r in range(REP):
            piece = value[:, r * HD : (r + 1) * HD]
            q_s[a, r * HD : (r + 1) * HD, :] = piece.astype(BF16)
            q_t[a, :HD, r * HD : (r + 1) * HD] = piece.T.astype(BF16)
        docs = jnp.concatenate([metas[z * NX + a, 0:1, :]] * REP, axis=1)
        other = lax.broadcasted_iota(jnp.int32, (HD, LANES), 0) != docs
        q_t[a, HD:, :] = jnp.where(other, -1e30, 0.0).astype(BF16)
        top[a] = jnp.full((1, LANES), -1e30, F32)
        total[a] = jnp.zeros((1, LANES), F32)
        acc_t[a] = jnp.zeros((HD, LANES), F32)
        return 0

    lax.fori_loop(0, NX, place_queries, 0)

    def place_keys(s, at, size):
        hit, is_image = chosen(base + (s - (WIN - 1)) * ROW + at, size)
        picked = jnp.dot(hit.astype(BF16), adapted[:, QC:], preferred_element_type=F32)
        both = jnp.where(is_image > 0.0, picked, kvw[s, at : at + size].astype(F32))
        ks[s, at : at + size, :HD] = both[:, :HD].astype(BF16)
        for j in range(at // TOK, (at + size) // TOK):
            same = lax.broadcasted_iota(jnp.int32, (HD, TOK), 0) == metas[(z + s - (WIN - 1)) * NX + j, 0:1, :]
            ks[s, j * TOK : (j + 1) * TOK, HD:] = jnp.where(same, 1.0, 0.0).astype(F32).T.astype(BF16)
        vs[s, at : at + size, :] = both[:, HD:].astype(BF16)
        kts[s, :, at : at + size] = both[:, :HD].T.astype(BF16)
        vts[s, :, at : at + size] = both[:, HD:].T.astype(BF16)

    within = lax.broadcasted_iota(jnp.int32, (1, TOK), 1)
    within = jnp.concatenate([within] * REP, axis=1)

    def forward(s, a, at, size, keep_prob, diagonal):
        value = jnp.dot(ks[s, at : at + size, :], q_t[a], preferred_element_type=F32)
        if diagonal:
            key_at = at + lax.broadcasted_iota(jnp.int32, (size, 1), 0)
            value = jnp.where(key_at <= a * TOK + within, value, -1e30)
        old = top[a]
        new = jnp.maximum(old, jnp.max(value, axis=0, keepdims=True))
        top[a] = new
        tops[s, a] = new
        factor = jnp.exp2((old - new) * (SCALE * LOG2E))
        prob = jnp.exp2((value - new) * (SCALE * LOG2E))
        total[a] = total[a] * factor + jnp.sum(prob, axis=0, keepdims=True)
        prob_b = prob.astype(BF16)
        keep_prob(prob_b)
        acc_t[a] = acc_t[a] * factor + jnp.dot(vts[s, :, at : at + size], prob_b, preferred_element_type=F32)

    place_keys(WIN - 1, 0, ROW)

    def forward_own(a, _):
        pass_keys(3, a)

        def keep_prob(prob):
            p_buf[WIN - 2, a] = prob

        forward(WIN - 1, a, 0, ROW, keep_prob, True)
        return 0

    lax.fori_loop(0, NX, forward_own, 0)

    def forward_row(k, _):
        s = WIN - 1 - k
        place_keys(s, 0, ROW)

        def one(a, _):
            @pl.when(k == 1)
            def _():
                pass_keys(4, a)

            def keep_prob(prob):
                p_buf[s - 1, a] = prob

            forward(s, a, 0, ROW, keep_prob, False)
            return 0

        lax.fori_loop(0, NX, one, 0)
        return 0

    lax.fori_loop(1, jnp.minimum(z + 1, 5), forward_row, 0)

    @pl.when(z >= WIN - 1)
    def _():
        hop(4, NX - 1).wait_recv()
        place_keys(0, ROW - TOK, TOK)

        def keep_prob(prob):
            p_first[...] = prob

        forward(0, 0, ROW - TOK, TOK, keep_prob, False)

    arrived_x(5)

    def send_turn(i, k, src, columns):
        peer = (x + i + 1) % NX

        @pl.when(i < NX - 1)
        def _():
            at = jnp.minimum(i, NX - 2)
            remote(src.at[peer], columns, x_send.at[at, k], x_recv.at[at, k], ctx_of(z, peer)).start()

        @pl.when(i == NX - 1)
        def _():
            own_x[k].start()

    def finish(i, _):
        a = (x + i + 1) % NX
        for r in range(REP):
            piece = do_in[a, :, r * HD : (r + 1) * HD]
            do_s[a, r * HD : (r + 1) * HD, :] = piece
            do_t[a, :, r * HD : (r + 1) * HD] = piece.astype(F32).T.astype(BF16)
        inverse = 1.0 / total[a]
        total[a] = inverse
        out_t = (acc_t[a] * inverse).astype(BF16).astype(F32)
        corr[a] = jnp.sum(do_t[a].astype(F32) * out_t, axis=0, keepdims=True)
        for r in range(REP):
            attn[a, :, r * HD : (r + 1) * HD] = out_t[:, r * HD : (r + 1) * HD].T.astype(BF16)
        acc_t[a] = jnp.zeros((HD, LANES), F32)
        send_turn(i, 6, attn, attn_out.at[:, cols(x * QC, QC)])
        return 0

    lax.fori_loop(0, NX, finish, 0)

    def backward(s, a, at, size, prob_b):
        part = jnp.exp2((tops[s, a] - top[a]) * (SCALE * LOG2E)) * total[a]
        prob = prob_b.astype(F32) * part
        dprob = jnp.dot(vs[s, at : at + size, :], do_t[a], preferred_element_type=F32)
        dscore = (prob * (dprob - corr[a])).astype(BF16)
        acc_t[a] += jnp.dot(kts[s, :, at : at + size], dscore, preferred_element_type=F32)
        dk = jnp.dot(dscore, q_s[a], preferred_element_type=F32)
        dv = jnp.dot(prob.astype(BF16), do_s[a], preferred_element_type=F32)
        return dk, dv

    first = remote(first_out, first_in, ring_send.at[0, 0], ring_recv.at[0, 0], ctx_of(down, x))
    def ring(k, j):
        part = rows_of(j * TOK, TOK)
        return remote(
            ring_out.at[k, part], ring_in.at[k, part], ring_send.at[1 + k, j], ring_recv.at[1 + k, j], ctx_of(down, x)
        )

    @pl.when(z >= WIN - 1)
    def _():
        dk, dv = backward(0, 0, ROW - TOK, TOK, p_first[...])
        first_out[:, :HD] = (dk * SCALE).astype(BF16)
        first_out[:, HD:] = dv.astype(BF16)
        first.start()

    def backward_tile(s, a, begin):
        dk, dv = backward(s, a, 0, ROW, p_buf[s - 1, a])

        @pl.when(begin)
        def _():
            dkv[:, :HD] = dk
            dkv[:, HD:] = dv

        @pl.when(jnp.logical_not(begin))
        def _():
            dkv[:, :HD] += dk
            dkv[:, HD:] += dv

    def summed(s, j):
        part = rows_of(j * TOK, TOK)
        whole[part, :HD] = (dkv[part, :HD] * SCALE).astype(BF16)
        whole[part, HD:] = dkv[part, HD:].astype(BF16)

        def add(arrived):
            whole[part, :HD] = (dkv[part, :HD] * SCALE + arrived[:, :HD].astype(F32)).astype(BF16)
            whole[part, HD:] = (dkv[part, HD:] + arrived[:, HD:].astype(F32)).astype(BF16)

        @pl.when((z <= NZ - 2) & ((s >= 2) | (j == NX - 1)))
        def _():
            if s == 1:
                first.wait_recv()
                add(first_in[...])
            else:
                ring(s - 2, j).wait_recv()
                add(ring_in[s - 2, part, :])

        return part

    for s in range(1, WIN - 1):

        @pl.when(z >= WIN - 1 - s)
        def _():
            def one(a, _):
                backward_tile(s, a, a == 0)
                return 0

            lax.fori_loop(0, NX, one, 0)
            for j in range(NX):
                part = summed(s, j)
                ring_out[s - 1, part, :] = whole[part, :]
                ring(s - 1, j).start()

    def end(i, _):
        a = (x + i + 1) % NX
        backward_tile(WIN - 1, a, i == 0)
        kept = keep[rows_of(a * TOK, TOK), :]
        value = acc_t[a] * SCALE
        for r in range(REP):
            piece = value[:, r * HD : (r + 1) * HD].T.astype(BF16)
            q_s[a, r * HD : (r + 1) * HD, :] = piece
            dq[a, :, r * HD : (r + 1) * HD] = (piece.astype(F32) * kept).astype(BF16)
        send_turn(i, 7, dq, text_grad.at[:, cols(x * QC, QC)])
        return 0

    lax.fori_loop(0, NX, end, 0)

    def z_pieces(peer):
        return [
            (scatq.at[rows_of(peer * 32, 32)], rxq.at[z]),
            (scatkv.at[rows_of(peer * 32, 32)], rxkv.at[z]),
            (vec_z, r_z.at[z]),
        ]

    own_z = [pltpu.make_async_copy(src, dst, own_sem.at[12 + k]) for k, (src, dst) in enumerate(z_pieces(z))]
    sent_z = []
    for d in range(1, NZ):
        peer = (z + d) % NZ
        sent_z.append([
            remote(src, dst, z_send.at[d - 1, k], z_recv.at[d - 1, k], ctx_of(peer, x))
            for k, (src, dst) in enumerate(z_pieces(peer))
        ])

    def send_z(k):
        for d in range(NZ - 1):
            sent_z[d][k].start()
        own_z[k].start()

    def arrived_z(k):
        own_z[k].wait()
        for d in range(NZ - 1):
            sent_z[d][k].wait_recv()

    vec[...] = jnp.zeros_like(vec)
    for r in range(REP):
        at = slice(r * HD, (r + 1) * HD)
        grads = jnp.concatenate([q_s[a, at, :] for a in range(NX)], axis=0)
        scattered = jnp.dot(onehot_t[...], grads, preferred_element_type=F32)
        scatq[:, at] = scattered.astype(BF16)
        vec[r : r + 1, :] = jnp.sum(scattered * raw[:, at].astype(F32), axis=0, keepdims=True)
        vec[10 + r : 11 + r, :] = jnp.sum(scattered, axis=0, keepdims=True)
    send_z(0)

    for i in range(NX):
        j = (x + i + 1) % NX
        part = summed(WIN - 1, j)
        kept = keep[part, :]
        mkv[part, :HD] = (whole[part, :HD].astype(F32) * kept).astype(BF16)
        mkv[part, HD:] = (whole[part, HD:].astype(F32) * kept).astype(BF16)
        for k in (8, 9):
            if i < NX - 1:
                sent_x[i][k].start()
            else:
                own_x[k].start()
    scattered = jnp.dot(onehot_t[...], whole[...], preferred_element_type=F32)
    scatkv[...] = scattered.astype(BF16)
    send_z(1)
    scale_part = jnp.sum(scattered * raw[:, QC:].astype(F32), axis=0, keepdims=True)
    shift_part = jnp.sum(scattered, axis=0, keepdims=True)
    for k in range(2):
        vec[REP + k : REP + k + 1, :] = scale_part[:, k * HD : (k + 1) * HD]
        vec[10 + REP + k : 11 + REP + k, :] = shift_part[:, k * HD : (k + 1) * HD]
    own_dp = pltpu.make_async_copy(vec, r_dp.at[dp], own_sem.at[15])
    sent_dp = [
        remote(vec, r_dp.at[dp], dp_send.at[d - 1], dp_recv.at[d - 1], {"dp": (dp + d) % NDP}) for d in range(1, NDP)
    ]
    for copy in sent_dp:
        copy.start()
    own_dp.start()

    own_dp.wait()
    for copy in sent_dp:
        copy.wait_recv()
    value = r_dp[0]
    for k in range(1, NDP):
        value = value + r_dp[k]
    vec_z[...] = value
    send_z(2)

    arrived_z(0)
    arrived_z(1)
    slots_q = rxq[0].astype(F32)
    slots_kv = rxkv[0].astype(F32)
    for k in range(1, NZ):
        slots_q = slots_q + rxq[k].astype(F32)
        slots_kv = slots_kv + rxkv[k].astype(F32)
    grad = jnp.concatenate([slots_q, slots_kv], axis=1) * scale
    for k in range(NX):
        piece = grad[k * SLOTS : (k + 1) * SLOTS]
        igs[k] = jnp.concatenate([piece[:, :HALF], piece[:, HALF:]], axis=0).astype(BF16)
    send_x(10)

    arrived_z(2)
    value = r_z[0]
    for k in range(1, NZ):
        value = value + r_z[k]
    vec_x[...] = value
    send_x(11)
    arrived_x(11)
    for head in range(NX):
        for out, at in ((scale_out, 0), (shift_out, 10)):
            out[head * REP : (head + 1) * REP, :] = r_x[head, at : at + REP, :]
            out[NX * REP + head : NX * REP + head + 1, :] = r_x[head, at + REP : at + REP + 1, :]
            out[NX * (REP + 1) + head : NX * (REP + 1) + head + 1, :] = r_x[head, at + REP + 1 : at + REP + 2, :]
    arrived_x(10)
    for head in range(NX):
        key, val = NX * QC + head * HD, NX * (QC + HD) + head * HD
        both = image_out[head].astype(F32)
        both = jnp.concatenate([both[:SLOTS], both[SLOTS:]], axis=1).astype(BF16)
        image_grad[:, head * QC : (head + 1) * QC] = both[:, :QC]
        image_grad[:, key : key + HD] = both[:, QC : QC + HD]
        image_grad[:, val : val + HD] = both[:, QC + HD :]
    for k in range(6, 10):
        arrived_x(k)

    for k in range(4):

        @pl.when((z >= k) & (z <= NZ - 2))
        def _():
            for j in range(NX):
                if k == 0:
                    key_step(j, 0).wait_send()
                    key_step(j, 1).wait_send()
                else:
                    hop(k, j).wait_send()

        @pl.when(z >= k + 1)
        def _():
            for j in range(NX):
                ring(3 - k, j).wait_send()

    @pl.when((z >= 4) & (z <= NZ - 2))
    def _():
        hop(4, NX - 1).wait_send()

    @pl.when(z >= WIN - 1)
    def _():
        first.wait_send()

    for k in range(2):
        for d in range(NX):
            image_step(up, 0, d, k).wait_send()
            image_step(down, 1, d, k).wait_send()
    for group in sent_x + sent_z + ups[1:] + downs[1:]:
        for copy in group:
            copy.wait_send()
    for copy in sent_dp:
        copy.wait_send()


def land_kernel(*refs):
    half = len(refs) // 2
    sems = refs[-1]
    copies = [pltpu.make_async_copy(refs[k], refs[half + k], sems.at[k]) for k in range(half)]
    for copy in copies:
        copy.start()
    for copy in copies:
        copy.wait()


def shape(dims, kind):
    return jax.ShapeDtypeStruct(dims, kind)


ANY = pl.BlockSpec(memory_space=pl.ANY)
VMEM = pl.BlockSpec(memory_space=pltpu.VMEM)
DMA = pltpu.SemaphoreType.DMA
LIMIT = 60 * 1024 * 1024


def per_device(
    text_rows, image_rows, tile_counts, tile_offsets, doc_ids, out_grad, proj_scale, proj_shift
):
    attn_out, text_grad, image_grad, scale_grad, shift_grad = pl.pallas_call(
        layer_kernel,
        out_shape=(
            shape((TOK, NX * QC), BF16),
            shape((TOK, NX * HC), BF16),
            shape((SLOTS, NX * HC), BF16),
            shape((NX * HC // HD, HD), F32),
            shape((NX * HC // HD, HD), F32),
        ),
        in_specs=[ANY, ANY] + [VMEM] * 6,
        out_specs=(ANY, ANY, VMEM, VMEM, VMEM),
        scratch_shapes=[
            pltpu.VMEM((NX, 16, HALF), BF16),
            pltpu.VMEM((8, TOK), jnp.int32),
            pltpu.VMEM((NX, 16, HALF), BF16),
            pltpu.VMEM((NX, TOK, QC), BF16),
            pltpu.VMEM((NX, TOK, QC), BF16),
            pltpu.VMEM((WIN, ROW, 2 * HD), BF16),
            pltpu.VMEM((NZ * NX, 16, HALF), BF16),
            pltpu.VMEM((NZ * NX, 8, TOK), jnp.int32),
            pltpu.VMEM((NSLOT, HC), BF16),
            pltpu.VMEM((NSLOT, HC), BF16),
            pltpu.VMEM((NSLOT, ROW), BF16),
            pltpu.VMEM((ROW, HD), F32),
            pltpu.VMEM((NX, 2 * HD, LANES), BF16),
            pltpu.VMEM((NX, HD, LANES), BF16),
            pltpu.VMEM((NX, LANES, HD), BF16),
            pltpu.VMEM((NX, LANES, HD), BF16),
            pltpu.VMEM((WIN, ROW, 2 * HD), BF16),
            pltpu.VMEM((WIN, ROW, HD), BF16),
            pltpu.VMEM((WIN, HD, ROW), BF16),
            pltpu.VMEM((WIN, HD, ROW), BF16),
            pltpu.VMEM((WIN - 1, NX, ROW, LANES), BF16),
            pltpu.VMEM((TOK, LANES), BF16),
            pltpu.VMEM((NX, HD, LANES), F32),
            pltpu.VMEM((NX, 1, LANES), F32),
            pltpu.VMEM((NX, 1, LANES), F32),
            pltpu.VMEM((WIN, NX, 1, LANES), F32),
            pltpu.VMEM((NX, 1, LANES), F32),
            pltpu.VMEM((ROW, 2 * HD), F32),
            pltpu.VMEM((NX, TOK, QC), BF16),
            pltpu.VMEM((NX, TOK, QC), BF16),
            pltpu.VMEM((TOK, 2 * HD), BF16),
            pltpu.VMEM((TOK, 2 * HD), BF16),
            pltpu.VMEM((4, ROW, 2 * HD), BF16),
            pltpu.VMEM((4, ROW, 2 * HD), BF16),
            pltpu.VMEM((ROW, 2 * HD), BF16),
            pltpu.VMEM((ROW, 2 * HD), BF16),
            pltpu.VMEM((NSLOT, QC), BF16),
            pltpu.VMEM((NSLOT, 2 * HD), BF16),
            pltpu.VMEM((NZ, 32, QC), BF16),
            pltpu.VMEM((NZ, 32, 2 * HD), BF16),
            pltpu.VMEM((NX, 16, HALF), BF16),
            pltpu.VMEM((24, HD), F32),
            pltpu.VMEM((24, HD), F32),
            pltpu.VMEM((24, HD), F32),
            pltpu.VMEM((NDP, 24, HD), F32),
            pltpu.VMEM((NZ, 24, HD), F32),
            pltpu.VMEM((NX, 24, HD), F32),
            DMA((2, 4, 2)), DMA((2, 4, 2)), DMA((4, 2)), DMA((4, 2)),
            DMA((16,)), DMA((3, 12)), DMA((3, 12)), DMA((5, 4)), DMA((5, 4)),
            DMA((3, 2)), DMA((3, 2)), DMA((4, 2)), DMA((4, 2)),
            DMA((5, 4)), DMA((5, 4)), DMA((7, 3)), DMA((7, 3)), DMA((7,)), DMA((7,)),
        ],
        compiler_params=pltpu.CompilerParams(
            collective_id=0, has_side_effects=True, vmem_limit_bytes=LIMIT
        ),
        name="layer",
    )(
        text_rows[0], out_grad[0], image_rows[0], tile_counts, tile_offsets, doc_ids,
        proj_scale.reshape(NX * HC // HD, HD), proj_shift.reshape(NX * HC // HD, HD),
    )
    results = (attn_out, text_grad, image_grad, scale_grad, shift_grad)
    attn_out, text_grad, image_grad, scale_grad, shift_grad = pl.pallas_call(
        land_kernel,
        out_shape=tuple(shape(a.shape, a.dtype) for a in results),
        in_specs=[VMEM] * 5,
        out_specs=(ANY,) * 5,
        scratch_shapes=[DMA((5,))],
        name="land",
    )(*results)
    return (
        attn_out[None], text_grad[None], image_grad[None],
        scale_grad.reshape(NX * HC), shift_grad.reshape(NX * HC),
    )


def solution(mesh):
    return jax.shard_map(
        per_device,
        mesh=mesh,
        in_specs=(
            P("dp", "ctx", None),
            P("dp", "ctx", None),
            P("dp", "ctx"),
            P("dp", "ctx"),
            P("dp", "ctx"),
            P("dp", "ctx", None),
            P(),
            P(),
        ),
        out_specs=(P("dp", "ctx", None), P("dp", "ctx", None), P("dp", "ctx", None), P(), P()),
        check_vma=False,
    )
```

```python
import math

import jax
import jax.numpy as jnp
from jax import lax
from jax.experimental import pallas as pl
from jax.experimental.pallas import tpu as pltpu
from jax.sharding import PartitionSpec as P

MESH = pl.DeviceIdType.MESH
HD = 128
REP = 8
DOCS = 8
NZ = 8
NX = 4
NDP = 8
TOK = 128
ROW = NX * TOK
SLOTS = 8
NSLOT = NZ * NX * SLOTS
QC = REP * HD
HC = QC + 2 * HD
WIN = 6
HALF = HC // 2
LANES = REP * TOK
SCALE = HD ** -0.5
LOG2E = math.log2(math.e)
F32 = jnp.float32
BF16 = jnp.bfloat16


def place():
    ctx = lax.axis_index("ctx")
    return lax.axis_index("dp"), ctx // NX, ctx % NX


def ctx_of(z, x):
    return {"ctx": z * NX + x}


def remote(src, dst, send, recv, device):
    return pltpu.make_async_remote_copy(
        src_ref=src, dst_ref=dst, send_sem=send, recv_sem=recv, device_id=device, device_id_type=MESH
    )


def cols(start, size):
    return pl.ds(pl.multiple_of(start, HD), size)


def rows_of(start, size):
    return pl.ds(pl.multiple_of(start, size), size)


def greet(devices):
    barrier = pltpu.get_barrier_semaphore()
    for device in devices:
        pl.semaphore_signal(barrier, inc=1, device_id=device, device_id_type=MESH)
    pl.semaphore_wait(barrier, len(devices))


def layer_kernel(
    text, dout, image_rows, counts, offsets, doc_ids, proj_scale, proj_shift,
    attn_out, text_grad, image_grad, scale_out, shift_out,
    image, meta, image_out, q_in, do_in, kvw, images, metas, raw, adapted, onehot_t, keep,
    q_t, do_t, q_s, do_s, ks, vs, kts, vts, p_buf, p_first, acc_t, top, total, tops, corr, dkv,
    attn, dq, first_in, first_out, ring_in, ring_out, whole, mkv, scatq, scatkv, rxq, rxkv, igs,
    vec, vec_z, vec_x, r_dp, r_z, r_x,
    img_send, img_recv, key_send, key_recv, own_sem, x_send, x_recv, kv_send, kv_recv, up_send, up_recv, down_send, down_recv,
    ring_send, ring_recv, z_send, z_recv, dp_send, dp_recv,
):
    dp, z, x = place()
    up, down = (z + 1) % NZ, (z + NZ - 1) % NZ
    me = z * NX + x
    base = z * ROW

    def of_head(ref, head):
        parts = [ref[pl.ds(head * REP + r, 1), :] for r in range(REP)]
        parts += [ref[pl.ds(NX * REP + head, 1), :], ref[pl.ds(NX * (REP + 1) + head, 1), :]]
        return jnp.concatenate(parts, axis=1)

    for head in range(NX):
        key, val = NX * QC + head * HD, NX * (QC + HD) + head * HD
        both = jnp.concatenate(
            [image_rows[:, head * QC : (head + 1) * QC], image_rows[:, key : key + HD], image_rows[:, val : val + HD]],
            axis=1,
        ).astype(F32)
        image[head] = jnp.concatenate([both[:, :HALF], both[:, HALF:]], axis=0).astype(BF16)
    lane = lax.broadcasted_iota(jnp.int32, (8, TOK), 1) - SLOTS * (me % 16)
    row = lax.broadcasted_iota(jnp.int32, (8, TOK), 0)
    live = (lane >= 0) & (lane < counts[...])
    filled = jnp.where(live, offsets[...] + lane + 1, 0)
    meta[...] = jnp.where(row == 0, doc_ids[...], jnp.where(row == 1 + me // 16, filled, 0))
    greet(
        [ctx_of(z, (x + d) % NX) for d in range(1, NX)]
        + [ctx_of((z + d) % NZ, x) for d in range(1, NZ)]
        + [{"dp": (dp + d) % NDP} for d in range(1, NDP)]
        + [ctx_of(near, (x + d) % NX) for near in (up, down) for d in range(1, NX)]
    )

    def pieces(peer):
        own_rows = rows_of(x * TOK, TOK)
        return [
            (meta, metas.at[me]),
            (image.at[peer], images.at[me]),
            (text.at[:, cols(NX * QC + peer * HD, HD)], kvw.at[WIN - 1, own_rows, pl.ds(0, HD)]),
            (text.at[:, cols(NX * QC + (NX + peer) * HD, HD)], kvw.at[WIN - 1, own_rows, pl.ds(HD, HD)]),
            (text.at[:, cols(peer * QC, QC)], q_in.at[x]),
            (dout.at[:, cols(peer * QC, QC)], do_in.at[x]),
            (attn.at[peer], attn_out.at[:, cols(x * QC, QC)]),
            (dq.at[peer], text_grad.at[:, cols(x * QC, QC)]),
            (mkv.at[rows_of(peer * TOK, TOK), pl.ds(0, HD)], text_grad.at[:, cols(NX * QC + x * HD, HD)]),
            (mkv.at[rows_of(peer * TOK, TOK), pl.ds(HD, HD)], text_grad.at[:, cols(NX * QC + (NX + x) * HD, HD)]),
            (igs.at[peer], image_out.at[x]),
            (vec_x, r_x.at[x]),
        ]

    own_x = [pltpu.make_async_copy(src, dst, own_sem.at[k]) for k, (src, dst) in enumerate(pieces(x))]
    sent_x = []
    for d in range(1, NX):
        peer = (x + d) % NX
        sent_x.append([
            remote(src, dst, x_send.at[d - 1, k], x_recv.at[d - 1, k], ctx_of(z, peer))
            for k, (src, dst) in enumerate(pieces(peer))
        ])

    def send_x(k):
        for d in range(NX - 1):
            sent_x[d][k].start()
        own_x[k].start()

    def arrived_x(k):
        own_x[k].wait()
        for d in range(NX - 1):
            sent_x[d][k].wait_recv()

    def image_step(near, way, d, k):
        head = (x + d) % NX
        src, dst = pieces(head)[k]
        return remote(src, dst, img_send.at[way, d, k], img_recv.at[way, x, k], ctx_of(near, head))

    def image_came(near, way, j, k):
        src, dst = pieces(j)[k]
        return remote(src, dst, img_send.at[way, 0, k], img_recv.at[way, j, k], ctx_of(near, j))

    def key_step(d, k):
        head = (x + d) % NX
        at = kvw.at[WIN - 2, rows_of(x * TOK, TOK), pl.ds(k * HD, HD)]
        src = text.at[:, cols(NX * QC + (NX * k + head) * HD, HD)]
        return remote(src, at, key_send.at[d, k], key_recv.at[x, k], ctx_of(up, head))

    def key_came(j, k):
        at = kvw.at[WIN - 2, rows_of(j * TOK, TOK), pl.ds(k * HD, HD)]
        src = text.at[:, cols(NX * QC + NX * k * HD, HD)]
        return remote(src, at, key_send.at[0, k], key_recv.at[j, k], ctx_of(up, x))

    send_x(0)
    send_x(1)
    for k in range(2):
        for d in range(NX):
            image_step(up, 0, d, k).start()
            image_step(down, 1, d, k).start()
    send_x(2)
    send_x(3)
    send_x(4)

    ups, downs = [None], [None]
    for k in range(1, 3):
        block = pl.ds(((z + NZ - k) % NZ) * NX, NX)
        ups.append([
            remote(a.at[block], a.at[block], up_send.at[k, j], up_recv.at[k, j], ctx_of(up, x))
            for j, a in enumerate((metas, images))
        ])
    for k in range(1, 4):
        block = pl.ds(((z + k) % NZ) * NX, NX)
        downs.append([
            remote(a.at[block], a.at[block], down_send.at[k, j], down_recv.at[k, j], ctx_of(down, x))
            for j, a in enumerate((metas, images))
        ])

    def hop(k, j):
        part = rows_of(j * TOK, TOK)
        return remote(
            kvw.at[WIN - 1 - k, part], kvw.at[WIN - 2 - k, part], kv_send.at[k, j], kv_recv.at[k, j], ctx_of(up, x)
        )

    def pass_keys(k, j):
        @pl.when(z >= k)
        def _():
            if k == 1:
                key_came(j, 0).wait_recv()
                key_came(j, 1).wait_recv()
            else:
                hop(k - 1, j).wait_recv()

        @pl.when((z >= k) & (z <= NZ - 2) & ((k < 4) | (j == NX - 1)))
        def _():
            hop(k, j).start()

    def pass_images(k):
        for j in range(2):
            if k == 1:
                for d in range(NX):
                    image_came(up, 0, d, j).wait_recv()
            elif k <= 3:
                ups[k - 1][j].wait_recv()
            if k < 3:
                ups[k][j].start()
            if k == 1:
                for d in range(NX):
                    image_came(down, 1, d, j).wait_recv()
            else:
                downs[k - 1][j].wait_recv()
            if k < 4:
                downs[k][j].start()

    pass_images(1)

    @pl.when(z <= NZ - 2)
    def _():
        for d in range(NX):
            for k in range(2):
                key_step(d, k).start()

    pass_images(2)
    for j in range(NX):
        pass_keys(1, j)
    pass_images(3)
    for k in range(4):
        arrived_x(k)
    pass_images(4)
    for j in range(NX):
        pass_keys(2, j)

    scale = of_head(proj_scale, x)
    shift = of_head(proj_shift, x)

    def adapt(pair, _):
        first = images[2 * pair].astype(F32)
        second = images[2 * pair + 1].astype(F32)
        left = jnp.concatenate([first[:8], second[:8]], axis=0)
        right = jnp.concatenate([first[8:], second[8:]], axis=0)
        at = rows_of(pair * 16, 16)
        raw[at, pl.ds(0, HALF)] = left.astype(BF16)
        raw[at, pl.ds(HALF, HALF)] = right.astype(BF16)
        adapted[at, pl.ds(0, HALF)] = (left * scale[:, :HALF] + shift[:, :HALF]).astype(BF16)
        adapted[at, pl.ds(HALF, HALF)] = (right * scale[:, HALF:] + shift[:, HALF:]).astype(BF16)
        return 0

    lax.fori_loop(0, NSLOT // 16, adapt, 0)
    all_metas = jnp.sum(metas[:, 1:3, :], axis=0)
    target = jnp.concatenate([all_metas[0:1], all_metas[1:2]], axis=1) - 1
    def chosen(begin, size):
        position = begin + lax.broadcasted_iota(jnp.int32, (size, NSLOT), 0)
        hit = jnp.where(position == target, 1.0, 0.0).astype(F32)
        return hit, jnp.max(hit, axis=1, keepdims=True)

    arrived_x(4)
    send_x(5)

    def place_queries(a, _):
        hit, is_image = chosen(base + a * TOK, TOK)
        onehot_t[:, cols(a * TOK, TOK)] = hit.T.astype(BF16)
        keep[rows_of(a * TOK, TOK), :] = jnp.broadcast_to(1.0 - is_image, (TOK, HD))
        picked = jnp.dot(hit.astype(BF16), adapted[:, :QC], preferred_element_type=F32)
        value = jnp.where(is_image > 0.0, picked, q_in[a].astype(F32))
        for r in range(REP):
            piece = value[:, r * HD : (r + 1) * HD]
            q_s[a, r * HD : (r + 1) * HD, :] = piece.astype(BF16)
            q_t[a, :HD, r * HD : (r + 1) * HD] = piece.T.astype(BF16)
        docs = jnp.concatenate([metas[z * NX + a, 0:1, :]] * REP, axis=1)
        other = lax.broadcasted_iota(jnp.int32, (HD, LANES), 0) != docs
        q_t[a, HD:, :] = jnp.where(other, -1e30, 0.0).astype(BF16)
        top[a] = jnp.full((1, LANES), -1e30, F32)
        total[a] = jnp.zeros((1, LANES), F32)
        acc_t[a] = jnp.zeros((HD, LANES), F32)
        return 0

    lax.fori_loop(0, NX, place_queries, 0)

    def place_keys(s, at, size):
        hit, is_image = chosen(base + (s - (WIN - 1)) * ROW + at, size)
        picked = jnp.dot(hit.astype(BF16), adapted[:, QC:], preferred_element_type=F32)
        both = jnp.where(is_image > 0.0, picked, kvw[s, at : at + size].astype(F32))
        ks[s, at : at + size, :HD] = both[:, :HD].astype(BF16)
        for j in range(at // TOK, (at + size) // TOK):
            same = lax.broadcasted_iota(jnp.int32, (HD, TOK), 0) == metas[(z + s - (WIN - 1)) * NX + j, 0:1, :]
            ks[s, j * TOK : (j + 1) * TOK, HD:] = jnp.where(same, 1.0, 0.0).astype(F32).T.astype(BF16)
        vs[s, at : at + size, :] = both[:, HD:].astype(BF16)
        kts[s, :, at : at + size] = both[:, :HD].T.astype(BF16)
        vts[s, :, at : at + size] = both[:, HD:].T.astype(BF16)

    within = lax.broadcasted_iota(jnp.int32, (1, TOK), 1)
    within = jnp.concatenate([within] * REP, axis=1)

    def forward(s, a, at, size, keep_prob, diagonal):
        lanes = [slice(k * 2 * HD, (k + 1) * 2 * HD) for k in range(LANES // (2 * HD))]
        values = [jnp.dot(ks[s, at : at + size, :], q_t[a, :, ln], preferred_element_type=F32) for ln in lanes]
        for value, ln in zip(values, lanes):
            if diagonal:
                key_at = at + lax.broadcasted_iota(jnp.int32, (size, 1), 0)
                value = jnp.where(key_at <= a * TOK + within[:, ln], value, -1e30)
            old = top[a, :, ln]
            new = jnp.maximum(old, jnp.max(value, axis=0, keepdims=True))
            top[a, :, ln] = new
            tops[s, a, :, ln] = new
            factor = jnp.exp2((old - new) * (SCALE * LOG2E))
            prob = jnp.exp2((value - new) * (SCALE * LOG2E))
            total[a, :, ln] = total[a, :, ln] * factor + jnp.sum(prob, axis=0, keepdims=True)
            prob_b = prob.astype(BF16)
            keep_prob(prob_b, ln)
            acc_t[a, :, ln] = acc_t[a, :, ln] * factor + jnp.dot(
                vts[s, :, at : at + size], prob_b, preferred_element_type=F32
            )

    place_keys(WIN - 1, 0, ROW)

    for a in range(NX):
        pass_keys(3, a)

        def keep_own(prob, ln):
            p_buf[WIN - 2, a, : (a + 1) * TOK, ln] = prob

        forward(WIN - 1, a, 0, (a + 1) * TOK, keep_own, True)

    def forward_row(k, _):
        s = WIN - 1 - k
        place_keys(s, 0, ROW)

        def one(a, _):
            @pl.when(k == 2)
            def _():
                pass_keys(4, a)

            def keep_prob(prob, ln):
                p_buf[s - 1, a, :, ln] = prob

            forward(s, a, 0, ROW, keep_prob, False)
            return 0

        lax.fori_loop(0, NX, one, 0)
        return 0

    lax.fori_loop(1, jnp.minimum(z + 1, 5), forward_row, 0)

    @pl.when(z >= WIN - 1)
    def _():
        hop(4, NX - 1).wait_recv()
        place_keys(0, ROW - TOK, TOK)

        def keep_prob(prob, ln):
            p_first[:, ln] = prob

        forward(0, 0, ROW - TOK, TOK, keep_prob, False)

    arrived_x(5)

    def send_turn(i, k, src, columns):
        peer = (x + i + 1) % NX

        @pl.when(i < NX - 1)
        def _():
            at = jnp.minimum(i, NX - 2)
            remote(src.at[peer], columns, x_send.at[at, k], x_recv.at[at, k], ctx_of(z, peer)).start()

        @pl.when(i == NX - 1)
        def _():
            own_x[k].start()

    def finish(i, _):
        a = (x + i + 1) % NX
        for r in range(REP):
            piece = do_in[a, :, r * HD : (r + 1) * HD]
            do_s[a, r * HD : (r + 1) * HD, :] = piece
            do_t[a, :, r * HD : (r + 1) * HD] = piece.astype(F32).T.astype(BF16)
        inverse = 1.0 / total[a]
        total[a] = inverse
        out_t = (acc_t[a] * inverse).astype(BF16).astype(F32)
        corr[a] = jnp.sum(do_t[a].astype(F32) * out_t, axis=0, keepdims=True)
        for r in range(REP):
            attn[a, :, r * HD : (r + 1) * HD] = out_t[:, r * HD : (r + 1) * HD].T.astype(BF16)
        acc_t[a] = jnp.zeros((HD, LANES), F32)
        send_turn(i, 6, attn, attn_out.at[:, cols(x * QC, QC)])
        return 0

    lax.fori_loop(0, NX, finish, 0)

    def backward(s, a, at, size, prob_b):
        part = jnp.exp2((tops[s, a] - top[a]) * (SCALE * LOG2E)) * total[a]
        prob = prob_b.astype(F32) * part
        dprob = jnp.dot(vs[s, at : at + size, :], do_t[a], preferred_element_type=F32)
        dscore = (prob * (dprob - corr[a])).astype(BF16)
        acc_t[a] += jnp.dot(kts[s, :, at : at + size], dscore, preferred_element_type=F32)
        dk = jnp.dot(dscore, q_s[a], preferred_element_type=F32)
        dv = jnp.dot(prob.astype(BF16), do_s[a], preferred_element_type=F32)
        return dk, dv

    first = remote(first_out, first_in, ring_send.at[0, 0], ring_recv.at[0, 0], ctx_of(down, x))
    def ring(k, j):
        part = rows_of(j * TOK, TOK)
        return remote(
            ring_out.at[k, part], ring_in.at[k, part], ring_send.at[1 + k, j], ring_recv.at[1 + k, j], ctx_of(down, x)
        )

    @pl.when(z >= WIN - 1)
    def _():
        dk, dv = backward(0, 0, ROW - TOK, TOK, p_first[...])
        first_out[:, :HD] = (dk * SCALE).astype(BF16)
        first_out[:, HD:] = dv.astype(BF16)
        first.start()

    def backward_tile(s, a, size):
        dk, dv = backward(s, a, 0, size, p_buf[s - 1, a, :size, :])
        dkv[s % 2, :size, :HD] += dk
        dkv[s % 2, :size, HD:] += dv

    def summed(s, j):
        part = rows_of(j * TOK, TOK)
        whole[part, :HD] = (dkv[s % 2, part, :HD] * SCALE).astype(BF16)
        whole[part, HD:] = dkv[s % 2, part, HD:].astype(BF16)

        def add(arrived):
            whole[part, :HD] = (dkv[s % 2, part, :HD] * SCALE + arrived[:, :HD].astype(F32)).astype(BF16)
            whole[part, HD:] = (dkv[s % 2, part, HD:] + arrived[:, HD:].astype(F32)).astype(BF16)

        @pl.when((z <= NZ - 2) & ((s >= 2) | (j == NX - 1)))
        def _():
            if s == 1:
                first.wait_recv()
                add(first_in[...])
            else:
                ring(s - 2, j).wait_recv()
                add(ring_in[s - 2, part, :])

        return part

    def pass_sums(s, j):
        part = summed(s, j)
        ring_out[s - 1, part, :] = whole[part, :]
        ring(s - 1, j).start()

    for s in range(1, WIN - 1):

        @pl.when(z >= WIN - 1 - s)
        def _():
            dkv[s % 2] = jnp.zeros((ROW, 2 * HD), F32)

            def one(a, _):
                backward_tile(s, a, ROW)
                if s >= 2:

                    @pl.when(z >= WIN - s)
                    def _():
                        pass_sums(s - 1, a)

                return 0

            lax.fori_loop(0, NX, one, 0)

    dkv[(WIN - 1) % 2] = jnp.zeros((ROW, 2 * HD), F32)

    def end(i, _):
        a = (x + i + 1) % NX
        for c in range(NX):

            @pl.when(a == c)
            def _():
                backward_tile(WIN - 1, c, (c + 1) * TOK)

        kept = keep[rows_of(a * TOK, TOK), :]
        value = acc_t[a] * SCALE
        for r in range(REP):
            piece = value[:, r * HD : (r + 1) * HD].T.astype(BF16)
            q_s[a, r * HD : (r + 1) * HD, :] = piece
            dq[a, :, r * HD : (r + 1) * HD] = (piece.astype(F32) * kept).astype(BF16)
        send_turn(i, 7, dq, text_grad.at[:, cols(x * QC, QC)])

        @pl.when(z >= 1)
        def _():
            pass_sums(WIN - 2, i)

        return 0

    lax.fori_loop(0, NX, end, 0)

    def z_pieces(peer):
        return [
            (scatq.at[rows_of(peer * 32, 32)], rxq.at[z]),
            (scatkv.at[rows_of(peer * 32, 32)], rxkv.at[z]),
            (vec_z, r_z.at[z]),
        ]

    own_z = [pltpu.make_async_copy(src, dst, own_sem.at[12 + k]) for k, (src, dst) in enumerate(z_pieces(z))]
    sent_z = []
    for d in range(1, NZ):
        peer = (z + d) % NZ
        sent_z.append([
            remote(src, dst, z_send.at[d - 1, k], z_recv.at[d - 1, k], ctx_of(peer, x))
            for k, (src, dst) in enumerate(z_pieces(peer))
        ])

    def send_z(k):
        for d in (3, 2, 4, 1, 5, 0, 6):
            sent_z[d][k].start()
        own_z[k].start()

    def arrived_z(k):
        own_z[k].wait()
        for d in range(NZ - 1):
            sent_z[d][k].wait_recv()

    vec[...] = jnp.zeros_like(vec)
    for r in range(REP):
        at = slice(r * HD, (r + 1) * HD)
        grads = jnp.concatenate([q_s[a, at, :] for a in range(NX)], axis=0)
        scattered = jnp.dot(onehot_t[...], grads, preferred_element_type=F32)
        scatq[:, at] = scattered.astype(BF16)
        vec[r : r + 1, :] = jnp.sum(scattered * raw[:, at].astype(F32), axis=0, keepdims=True)
        vec[10 + r : 11 + r, :] = jnp.sum(scattered, axis=0, keepdims=True)
    send_z(0)

    for i in range(NX):
        j = (x + i + 1) % NX
        part = summed(WIN - 1, j)
        kept = keep[part, :]
        mkv[part, :HD] = (whole[part, :HD].astype(F32) * kept).astype(BF16)
        mkv[part, HD:] = (whole[part, HD:].astype(F32) * kept).astype(BF16)
        for k in (8, 9):
            if i < NX - 1:
                sent_x[i][k].start()
            else:
                own_x[k].start()
    scattered = jnp.dot(onehot_t[...], whole[...], preferred_element_type=F32)
    scatkv[...] = scattered.astype(BF16)
    send_z(1)
    scale_part = jnp.sum(scattered * raw[:, QC:].astype(F32), axis=0, keepdims=True)
    shift_part = jnp.sum(scattered, axis=0, keepdims=True)
    for k in range(2):
        vec[REP + k : REP + k + 1, :] = scale_part[:, k * HD : (k + 1) * HD]
        vec[10 + REP + k : 11 + REP + k, :] = shift_part[:, k * HD : (k + 1) * HD]
    own_dp = pltpu.make_async_copy(vec, r_dp.at[dp], own_sem.at[15])
    sent_dp = [
        remote(vec, r_dp.at[dp], dp_send.at[d - 1], dp_recv.at[d - 1], {"dp": (dp + d) % NDP}) for d in range(1, NDP)
    ]
    for copy in sent_dp:
        copy.start()
    own_dp.start()

    own_dp.wait()
    for copy in sent_dp:
        copy.wait_recv()
    value = r_dp[0]
    for k in range(1, NDP):
        value = value + r_dp[k]
    vec_z[...] = value
    send_z(2)

    arrived_z(0)
    arrived_z(1)
    slots_q = rxq[0].astype(F32)
    slots_kv = rxkv[0].astype(F32)
    for k in range(1, NZ):
        slots_q = slots_q + rxq[k].astype(F32)
        slots_kv = slots_kv + rxkv[k].astype(F32)
    grad = jnp.concatenate([slots_q, slots_kv], axis=1) * scale
    for k in range(NX):
        piece = grad[k * SLOTS : (k + 1) * SLOTS]
        igs[k] = jnp.concatenate([piece[:, :HALF], piece[:, HALF:]], axis=0).astype(BF16)
    send_x(10)

    arrived_z(2)
    value = r_z[0]
    for k in range(1, NZ):
        value = value + r_z[k]
    vec_x[...] = value
    send_x(11)
    arrived_x(11)
    for head in range(NX):
        for out, at in ((scale_out, 0), (shift_out, 10)):
            out[head * REP : (head + 1) * REP, :] = r_x[head, at : at + REP, :]
            out[NX * REP + head : NX * REP + head + 1, :] = r_x[head, at + REP : at + REP + 1, :]
            out[NX * (REP + 1) + head : NX * (REP + 1) + head + 1, :] = r_x[head, at + REP + 1 : at + REP + 2, :]
    arrived_x(10)
    for head in range(NX):
        key, val = NX * QC + head * HD, NX * (QC + HD) + head * HD
        both = image_out[head].astype(F32)
        both = jnp.concatenate([both[:SLOTS], both[SLOTS:]], axis=1).astype(BF16)
        image_grad[:, head * QC : (head + 1) * QC] = both[:, :QC]
        image_grad[:, key : key + HD] = both[:, QC : QC + HD]
        image_grad[:, val : val + HD] = both[:, QC + HD :]
    for k in range(6, 10):
        arrived_x(k)

    for k in range(4):

        @pl.when((z >= k) & (z <= NZ - 2))
        def _():
            for j in range(NX):
                if k == 0:
                    key_step(j, 0).wait_send()
                    key_step(j, 1).wait_send()
                else:
                    hop(k, j).wait_send()

        @pl.when(z >= k + 1)
        def _():
            for j in range(NX):
                ring(3 - k, j).wait_send()

    @pl.when((z >= 4) & (z <= NZ - 2))
    def _():
        hop(4, NX - 1).wait_send()

    @pl.when(z >= WIN - 1)
    def _():
        first.wait_send()

    for k in range(2):
        for d in range(NX):
            image_step(up, 0, d, k).wait_send()
            image_step(down, 1, d, k).wait_send()
    for group in sent_x + sent_z + ups[1:] + downs[1:]:
        for copy in group:
            copy.wait_send()
    for copy in sent_dp:
        copy.wait_send()


def land_kernel(*refs):
    half = len(refs) // 2
    sems = refs[-1]
    copies = [pltpu.make_async_copy(refs[k], refs[half + k], sems.at[k]) for k in range(half)]
    for copy in copies:
        copy.start()
    for copy in copies:
        copy.wait()


def shape(dims, kind):
    return jax.ShapeDtypeStruct(dims, kind)


ANY = pl.BlockSpec(memory_space=pl.ANY)
VMEM = pl.BlockSpec(memory_space=pltpu.VMEM)
DMA = pltpu.SemaphoreType.DMA
LIMIT = 60 * 1024 * 1024


def per_device(
    text_rows, image_rows, tile_counts, tile_offsets, doc_ids, out_grad, proj_scale, proj_shift
):
    attn_out, text_grad, image_grad, scale_grad, shift_grad = pl.pallas_call(
        layer_kernel,
        out_shape=(
            shape((TOK, NX * QC), BF16),
            shape((TOK, NX * HC), BF16),
            shape((SLOTS, NX * HC), BF16),
            shape((NX * HC // HD, HD), F32),
            shape((NX * HC // HD, HD), F32),
        ),
        in_specs=[ANY, ANY] + [VMEM] * 6,
        out_specs=(ANY, ANY, VMEM, VMEM, VMEM),
        scratch_shapes=[
            pltpu.VMEM((NX, 16, HALF), BF16),
            pltpu.VMEM((8, TOK), jnp.int32),
            pltpu.VMEM((NX, 16, HALF), BF16),
            pltpu.VMEM((NX, TOK, QC), BF16),
            pltpu.VMEM((NX, TOK, QC), BF16),
            pltpu.VMEM((WIN, ROW, 2 * HD), BF16),
            pltpu.VMEM((NZ * NX, 16, HALF), BF16),
            pltpu.VMEM((NZ * NX, 8, TOK), jnp.int32),
            pltpu.VMEM((NSLOT, HC), BF16),
            pltpu.VMEM((NSLOT, HC), BF16),
            pltpu.VMEM((NSLOT, ROW), BF16),
            pltpu.VMEM((ROW, HD), F32),
            pltpu.VMEM((NX, 2 * HD, LANES), BF16),
            pltpu.VMEM((NX, HD, LANES), BF16),
            pltpu.VMEM((NX, LANES, HD), BF16),
            pltpu.VMEM((NX, LANES, HD), BF16),
            pltpu.VMEM((WIN, ROW, 2 * HD), BF16),
            pltpu.VMEM((WIN, ROW, HD), BF16),
            pltpu.VMEM((WIN, HD, ROW), BF16),
            pltpu.VMEM((WIN, HD, ROW), BF16),
            pltpu.VMEM((WIN - 1, NX, ROW, LANES), BF16),
            pltpu.VMEM((TOK, LANES), BF16),
            pltpu.VMEM((NX, HD, LANES), F32),
            pltpu.VMEM((NX, 1, LANES), F32),
            pltpu.VMEM((NX, 1, LANES), F32),
            pltpu.VMEM((WIN, NX, 1, LANES), F32),
            pltpu.VMEM((NX, 1, LANES), F32),
            pltpu.VMEM((2, ROW, 2 * HD), F32),
            pltpu.VMEM((NX, TOK, QC), BF16),
            pltpu.VMEM((NX, TOK, QC), BF16),
            pltpu.VMEM((TOK, 2 * HD), BF16),
            pltpu.VMEM((TOK, 2 * HD), BF16),
            pltpu.VMEM((4, ROW, 2 * HD), BF16),
            pltpu.VMEM((4, ROW, 2 * HD), BF16),
            pltpu.VMEM((ROW, 2 * HD), BF16),
            pltpu.VMEM((ROW, 2 * HD), BF16),
            pltpu.VMEM((NSLOT, QC), BF16),
            pltpu.VMEM((NSLOT, 2 * HD), BF16),
            pltpu.VMEM((NZ, 32, QC), BF16),
            pltpu.VMEM((NZ, 32, 2 * HD), BF16),
            pltpu.VMEM((NX, 16, HALF), BF16),
            pltpu.VMEM((24, HD), F32),
            pltpu.VMEM((24, HD), F32),
            pltpu.VMEM((24, HD), F32),
            pltpu.VMEM((NDP, 24, HD), F32),
            pltpu.VMEM((NZ, 24, HD), F32),
            pltpu.VMEM((NX, 24, HD), F32),
            DMA((2, 4, 2)), DMA((2, 4, 2)), DMA((4, 2)), DMA((4, 2)),
            DMA((16,)), DMA((3, 12)), DMA((3, 12)), DMA((5, 4)), DMA((5, 4)),
            DMA((3, 2)), DMA((3, 2)), DMA((4, 2)), DMA((4, 2)),
            DMA((5, 4)), DMA((5, 4)), DMA((7, 3)), DMA((7, 3)), DMA((7,)), DMA((7,)),
        ],
        compiler_params=pltpu.CompilerParams(
            collective_id=0, has_side_effects=True, vmem_limit_bytes=LIMIT
        ),
        name="layer",
    )(
        text_rows[0], out_grad[0], image_rows[0], tile_counts, tile_offsets, doc_ids,
        proj_scale.reshape(NX * HC // HD, HD), proj_shift.reshape(NX * HC // HD, HD),
    )
    results = (attn_out, text_grad, image_grad, scale_grad, shift_grad)
    attn_out, text_grad, image_grad, scale_grad, shift_grad = pl.pallas_call(
        land_kernel,
        out_shape=tuple(shape(a.shape, a.dtype) for a in results),
        in_specs=[VMEM] * 5,
        out_specs=(ANY,) * 5,
        scratch_shapes=[DMA((5,))],
        name="land",
    )(*results)
    return (
        attn_out[None], text_grad[None], image_grad[None],
        scale_grad.reshape(NX * HC), shift_grad.reshape(NX * HC),
    )


def solution(mesh):
    return jax.shard_map(
        per_device,
        mesh=mesh,
        in_specs=(
            P("dp", "ctx", None),
            P("dp", "ctx", None),
            P("dp", "ctx"),
            P("dp", "ctx"),
            P("dp", "ctx"),
            P("dp", "ctx", None),
            P(),
            P(),
        ),
        out_specs=(P("dp", "ctx", None), P("dp", "ctx", None), P("dp", "ctx", None), P(), P()),
        check_vma=False,
    )
```

```python
import math

import jax
import jax.numpy as jnp
from jax import lax
from jax.experimental import pallas as pl
from jax.experimental.pallas import tpu as pltpu
from jax.sharding import PartitionSpec as P

MESH = pl.DeviceIdType.MESH
HD = 128
REP = 8
DOCS = 8
NZ = 8
NX = 4
NDP = 8
TOK = 128
ROW = NX * TOK
SLOTS = 8
NSLOT = NZ * NX * SLOTS
QC = REP * HD
HC = QC + 2 * HD
WIN = 6
HALF = HC // 2
LANES = REP * TOK
SCALE = HD ** -0.5
LOG2E = math.log2(math.e)
F32 = jnp.float32
BF16 = jnp.bfloat16


def place():
    ctx = lax.axis_index("ctx")
    return lax.axis_index("dp"), ctx // NX, ctx % NX


def ctx_of(z, x):
    return {"ctx": z * NX + x}


def remote(src, dst, send, recv, device):
    return pltpu.make_async_remote_copy(
        src_ref=src, dst_ref=dst, send_sem=send, recv_sem=recv, device_id=device, device_id_type=MESH
    )


def cols(start, size):
    return pl.ds(pl.multiple_of(start, HD), size)


def rows_of(start, size):
    return pl.ds(pl.multiple_of(start, size), size)


def greet(devices):
    barrier = pltpu.get_barrier_semaphore()
    for device in devices:
        pl.semaphore_signal(barrier, inc=1, device_id=device, device_id_type=MESH)
    pl.semaphore_wait(barrier, len(devices))


def layer_kernel(
    text, dout, image_rows, counts, offsets, doc_ids, proj_scale, proj_shift,
    attn_out, text_grad, image_grad, scale_out, shift_out,
    image, meta, image_out, q_in, do_in, kvw, images, metas, raw, adapted, onehot_t, keep,
    q_t, do_t, q_s, do_s, ks, vs, kts, vts, p_buf, p_first, acc_t, top, total, tops, corr, dkv,
    attn, dq, first_in, first_out, ring_in, ring_out, whole, mkv, scatq, scatkv, rxq, rxkv, igs,
    vec, vec_z, vec_x, r_dp, r_z, r_x,
    img_send, img_recv, key_send, key_recv, own_sem, x_send, x_recv, kv_send, kv_recv, up_send, up_recv, down_send, down_recv,
    ring_send, ring_recv, z_send, z_recv, dp_send, dp_recv,
):
    dp, z, x = place()
    up, down = (z + 1) % NZ, (z + NZ - 1) % NZ
    me = z * NX + x
    base = z * ROW

    def of_head(ref, head):
        parts = [ref[pl.ds(head * REP + r, 1), :] for r in range(REP)]
        parts += [ref[pl.ds(NX * REP + head, 1), :], ref[pl.ds(NX * (REP + 1) + head, 1), :]]
        return jnp.concatenate(parts, axis=1)

    for head in range(NX):
        key, val = NX * QC + head * HD, NX * (QC + HD) + head * HD
        both = jnp.concatenate(
            [image_rows[:, head * QC : (head + 1) * QC], image_rows[:, key : key + HD], image_rows[:, val : val + HD]],
            axis=1,
        ).astype(F32)
        image[head] = jnp.concatenate([both[:, :HALF], both[:, HALF:]], axis=0).astype(BF16)
    lane = lax.broadcasted_iota(jnp.int32, (8, TOK), 1) - SLOTS * (me % 16)
    row = lax.broadcasted_iota(jnp.int32, (8, TOK), 0)
    live = (lane >= 0) & (lane < counts[...])
    filled = jnp.where(live, offsets[...] + lane + 1, 0)
    meta[...] = jnp.where(row == 0, doc_ids[...], jnp.where(row == 1 + me // 16, filled, 0))
    greet(
        [ctx_of(z, (x + d) % NX) for d in range(1, NX)]
        + [ctx_of((z + d) % NZ, x) for d in range(1, NZ)]
        + [{"dp": (dp + d) % NDP} for d in range(1, NDP)]
        + [ctx_of(near, (x + d) % NX) for near in (up, down) for d in range(1, NX)]
    )

    def pieces(peer):
        own_rows = rows_of(x * TOK, TOK)
        return [
            (meta, metas.at[me]),
            (image.at[peer], images.at[me]),
            (text.at[:, cols(NX * QC + peer * HD, HD)], kvw.at[WIN - 1, own_rows, pl.ds(0, HD)]),
            (text.at[:, cols(NX * QC + (NX + peer) * HD, HD)], kvw.at[WIN - 1, own_rows, pl.ds(HD, HD)]),
            (text.at[:, cols(peer * QC, QC)], q_in.at[x]),
            (dout.at[:, cols(peer * QC, QC)], do_in.at[x]),
            (attn.at[peer], attn_out.at[:, cols(x * QC, QC)]),
            (dq.at[peer], text_grad.at[:, cols(x * QC, QC)]),
            (mkv.at[rows_of(peer * TOK, TOK), pl.ds(0, HD)], text_grad.at[:, cols(NX * QC + x * HD, HD)]),
            (mkv.at[rows_of(peer * TOK, TOK), pl.ds(HD, HD)], text_grad.at[:, cols(NX * QC + (NX + x) * HD, HD)]),
            (igs.at[peer], image_out.at[x]),
            (vec_x, r_x.at[x]),
        ]

    own_x = [pltpu.make_async_copy(src, dst, own_sem.at[k]) for k, (src, dst) in enumerate(pieces(x))]
    sent_x = []
    for d in range(1, NX):
        peer = (x + d) % NX
        sent_x.append([
            remote(src, dst, x_send.at[d - 1, k], x_recv.at[d - 1, k], ctx_of(z, peer))
            for k, (src, dst) in enumerate(pieces(peer))
        ])

    def send_x(k):
        for d in range(NX - 1):
            sent_x[d][k].start()
        own_x[k].start()

    def arrived_x(k):
        own_x[k].wait()
        for d in range(NX - 1):
            sent_x[d][k].wait_recv()

    def image_step(near, way, d, k):
        head = (x + d) % NX
        src, dst = pieces(head)[k]
        return remote(src, dst, img_send.at[way, d, k], img_recv.at[way, x, k], ctx_of(near, head))

    def image_came(near, way, j, k):
        src, dst = pieces(j)[k]
        return remote(src, dst, img_send.at[way, 0, k], img_recv.at[way, j, k], ctx_of(near, j))

    def key_step(d, k):
        head = (x + d) % NX
        at = kvw.at[WIN - 2, rows_of(x * TOK, TOK), pl.ds(k * HD, HD)]
        src = text.at[:, cols(NX * QC + (NX * k + head) * HD, HD)]
        return remote(src, at, key_send.at[d, k], key_recv.at[x, k], ctx_of(up, head))

    def key_came(j, k):
        at = kvw.at[WIN - 2, rows_of(j * TOK, TOK), pl.ds(k * HD, HD)]
        src = text.at[:, cols(NX * QC + NX * k * HD, HD)]
        return remote(src, at, key_send.at[0, k], key_recv.at[j, k], ctx_of(up, x))

    send_x(0)
    send_x(1)
    for k in range(2):
        for d in range(NX):
            image_step(up, 0, d, k).start()
            image_step(down, 1, d, k).start()
    send_x(2)
    send_x(3)
    send_x(4)

    ups, downs = [None], [None]
    for k in range(1, 3):
        block = pl.ds(((z + NZ - k) % NZ) * NX, NX)
        ups.append([
            remote(a.at[block], a.at[block], up_send.at[k, j], up_recv.at[k, j], ctx_of(up, x))
            for j, a in enumerate((metas, images))
        ])
    for k in range(1, 4):
        block = pl.ds(((z + k) % NZ) * NX, NX)
        downs.append([
            remote(a.at[block], a.at[block], down_send.at[k, j], down_recv.at[k, j], ctx_of(down, x))
            for j, a in enumerate((metas, images))
        ])

    def hop(k, j):
        part = rows_of(j * TOK, TOK)
        return remote(
            kvw.at[WIN - 1 - k, part], kvw.at[WIN - 2 - k, part], kv_send.at[k, j], kv_recv.at[k, j], ctx_of(up, x)
        )

    def pass_keys(k, j):
        @pl.when(z >= k)
        def _():
            if k == 1:
                key_came(j, 0).wait_recv()
                key_came(j, 1).wait_recv()
            else:
                hop(k - 1, j).wait_recv()

        @pl.when((z >= k) & (z <= NZ - 2) & ((k < 4) | (j == NX - 1)))
        def _():
            hop(k, j).start()

    def pass_images(k):
        for j in range(2):
            if k == 1:
                for d in range(NX):
                    image_came(up, 0, d, j).wait_recv()
            elif k <= 3:
                ups[k - 1][j].wait_recv()
            if k < 3:
                ups[k][j].start()
            if k == 1:
                for d in range(NX):
                    image_came(down, 1, d, j).wait_recv()
            else:
                downs[k - 1][j].wait_recv()
            if k < 4:
                downs[k][j].start()

    pass_images(1)

    @pl.when(z <= NZ - 2)
    def _():
        for d in range(NX):
            for k in range(2):
                key_step(d, k).start()

    pass_images(2)
    for j in range(NX):
        pass_keys(1, j)
    pass_images(3)
    for k in range(4):
        arrived_x(k)
    for j in range(NX):
        pass_keys(2, j)
    pass_images(4)

    scale = of_head(proj_scale, x)
    shift = of_head(proj_shift, x)

    def adapt(pair, _):
        first = images[2 * pair].astype(F32)
        second = images[2 * pair + 1].astype(F32)
        left = jnp.concatenate([first[:8], second[:8]], axis=0)
        right = jnp.concatenate([first[8:], second[8:]], axis=0)
        at = rows_of(pair * 16, 16)
        raw[at, pl.ds(0, HALF)] = left.astype(BF16)
        raw[at, pl.ds(HALF, HALF)] = right.astype(BF16)
        adapted[at, pl.ds(0, HALF)] = (left * scale[:, :HALF] + shift[:, :HALF]).astype(BF16)
        adapted[at, pl.ds(HALF, HALF)] = (right * scale[:, HALF:] + shift[:, HALF:]).astype(BF16)
        return 0

    lax.fori_loop(0, NSLOT // 16, adapt, 0)
    all_metas = jnp.sum(metas[:, 1:3, :], axis=0)
    target = jnp.concatenate([all_metas[0:1], all_metas[1:2]], axis=1) - 1
    def chosen(begin, size):
        position = begin + lax.broadcasted_iota(jnp.int32, (size, NSLOT), 0)
        hit = jnp.where(position == target, 1.0, 0.0).astype(F32)
        return hit, jnp.max(hit, axis=1, keepdims=True)

    arrived_x(4)
    send_x(5)

    def place_queries(a, _):
        hit, is_image = chosen(base + a * TOK, TOK)
        onehot_t[:, cols(a * TOK, TOK)] = hit.T.astype(BF16)
        keep[rows_of(a * TOK, TOK), :] = jnp.broadcast_to(1.0 - is_image, (TOK, HD))
        picked = jnp.dot(hit.astype(BF16), adapted[:, :QC], preferred_element_type=F32)
        value = jnp.where(is_image > 0.0, picked, q_in[a].astype(F32))
        for r in range(REP):
            piece = value[:, r * HD : (r + 1) * HD]
            q_s[a, r * HD : (r + 1) * HD, :] = piece.astype(BF16)
            q_t[a, :HD, r * HD : (r + 1) * HD] = piece.T.astype(BF16)
        docs = jnp.concatenate([metas[z * NX + a, 0:1, :]] * REP, axis=1)
        other = lax.broadcasted_iota(jnp.int32, (HD, LANES), 0) != docs
        q_t[a, HD:, :] = jnp.where(other, -1e30, 0.0).astype(BF16)
        top[a] = jnp.full((1, LANES), -1e30, F32)
        total[a] = jnp.zeros((1, LANES), F32)
        acc_t[a] = jnp.zeros((HD, LANES), F32)
        return 0

    lax.fori_loop(0, NX, place_queries, 0)

    def place_keys(s, at, size):
        hit, is_image = chosen(base + (s - (WIN - 1)) * ROW + at, size)
        picked = jnp.dot(hit.astype(BF16), adapted[:, QC:], preferred_element_type=F32)
        both = jnp.where(is_image > 0.0, picked, kvw[s, at : at + size].astype(F32))
        ks[s, at : at + size, :HD] = both[:, :HD].astype(BF16)
        for j in range(at // TOK, (at + size) // TOK):
            same = lax.broadcasted_iota(jnp.int32, (HD, TOK), 0) == metas[(z + s - (WIN - 1)) * NX + j, 0:1, :]
            ks[s, j * TOK : (j + 1) * TOK, HD:] = jnp.where(same, 1.0, 0.0).astype(F32).T.astype(BF16)
        vs[s, at : at + size, :] = both[:, HD:].astype(BF16)
        kts[s, :, at : at + size] = both[:, :HD].T.astype(BF16)
        vts[s, :, at : at + size] = both[:, HD:].T.astype(BF16)

    within = lax.broadcasted_iota(jnp.int32, (1, TOK), 1)
    within = jnp.concatenate([within] * REP, axis=1)

    def forward(s, a, at, size, keep_prob, diagonal):
        lanes = [slice(k * 2 * HD, (k + 1) * 2 * HD) for k in range(LANES // (2 * HD))]
        values = [jnp.dot(ks[s, at : at + size, :], q_t[a, :, ln], preferred_element_type=F32) for ln in lanes]
        for value, ln in zip(values, lanes):
            if diagonal:
                key_at = at + lax.broadcasted_iota(jnp.int32, (size, 1), 0)
                value = jnp.where(key_at <= a * TOK + within[:, ln], value, -1e30)
            old = top[a, :, ln]
            new = jnp.maximum(old, jnp.max(value, axis=0, keepdims=True))
            top[a, :, ln] = new
            tops[s, a, :, ln] = new
            factor = jnp.exp2((old - new) * (SCALE * LOG2E))
            prob = jnp.exp2((value - new) * (SCALE * LOG2E))
            total[a, :, ln] = total[a, :, ln] * factor + jnp.sum(prob, axis=0, keepdims=True)
            prob_b = prob.astype(BF16)
            keep_prob(prob_b, ln)
            acc_t[a, :, ln] = acc_t[a, :, ln] * factor + jnp.dot(
                vts[s, :, at : at + size], prob_b, preferred_element_type=F32
            )

    place_keys(WIN - 1, 0, ROW)

    for a in range(NX):
        pass_keys(3, a)

        def keep_own(prob, ln):
            p_buf[WIN - 2, a, : (a + 1) * TOK, ln] = prob

        forward(WIN - 1, a, 0, (a + 1) * TOK, keep_own, True)

    def forward_row(k, _):
        s = WIN - 1 - k
        place_keys(s, 0, ROW)

        def one(a, _):
            @pl.when(k == 2)
            def _():
                pass_keys(4, a)

            def keep_prob(prob, ln):
                p_buf[s - 1, a, :, ln] = prob

            forward(s, a, 0, ROW, keep_prob, False)
            return 0

        lax.fori_loop(0, NX, one, 0)
        return 0

    lax.fori_loop(1, jnp.minimum(z + 1, 5), forward_row, 0)

    @pl.when(z >= WIN - 1)
    def _():
        hop(4, NX - 1).wait_recv()
        place_keys(0, ROW - TOK, TOK)

        def keep_prob(prob, ln):
            p_first[:, ln] = prob

        forward(0, 0, ROW - TOK, TOK, keep_prob, False)

    arrived_x(5)

    def send_turn(i, k, src, columns):
        peer = (x + i + 1) % NX

        @pl.when(i < NX - 1)
        def _():
            at = jnp.minimum(i, NX - 2)
            remote(src.at[peer], columns, x_send.at[at, k], x_recv.at[at, k], ctx_of(z, peer)).start()

        @pl.when(i == NX - 1)
        def _():
            own_x[k].start()

    def finish(i, _):
        a = (x + i + 1) % NX
        for r in range(REP):
            piece = do_in[a, :, r * HD : (r + 1) * HD]
            do_s[a, r * HD : (r + 1) * HD, :] = piece
            do_t[a, :, r * HD : (r + 1) * HD] = piece.astype(F32).T.astype(BF16)
        inverse = 1.0 / total[a]
        total[a] = inverse
        out_t = (acc_t[a] * inverse).astype(BF16).astype(F32)
        corr[a] = jnp.sum(do_t[a].astype(F32) * out_t, axis=0, keepdims=True)
        for r in range(REP):
            attn[a, :, r * HD : (r + 1) * HD] = out_t[:, r * HD : (r + 1) * HD].T.astype(BF16)
        acc_t[a] = jnp.zeros((HD, LANES), F32)
        send_turn(i, 6, attn, attn_out.at[:, cols(x * QC, QC)])
        return 0

    lax.fori_loop(0, NX, finish, 0)

    def backward(s, a, at, size, prob_b):
        part = jnp.exp2((tops[s, a] - top[a]) * (SCALE * LOG2E)) * total[a]
        prob = prob_b.astype(F32) * part
        dprob = jnp.dot(vs[s, at : at + size, :], do_t[a], preferred_element_type=F32)
        dscore = (prob * (dprob - corr[a])).astype(BF16)
        acc_t[a] += jnp.dot(kts[s, :, at : at + size], dscore, preferred_element_type=F32)
        dk = jnp.dot(dscore, q_s[a], preferred_element_type=F32)
        dv = jnp.dot(prob.astype(BF16), do_s[a], preferred_element_type=F32)
        return dk, dv

    first = remote(first_out, first_in, ring_send.at[0, 0], ring_recv.at[0, 0], ctx_of(down, x))
    def ring(k, j):
        part = rows_of(j * TOK, TOK)
        return remote(
            ring_out.at[k, part], ring_in.at[k, part], ring_send.at[1 + k, j], ring_recv.at[1 + k, j], ctx_of(down, x)
        )

    @pl.when(z >= WIN - 1)
    def _():
        dk, dv = backward(0, 0, ROW - TOK, TOK, p_first[...])
        first_out[:, :HD] = (dk * SCALE).astype(BF16)
        first_out[:, HD:] = dv.astype(BF16)
        first.start()

    def backward_tile(s, a, size):
        dk, dv = backward(s, a, 0, size, p_buf[s - 1, a, :size, :])
        dkv[s % 2, :size, :HD] += dk
        dkv[s % 2, :size, HD:] += dv

    def summed(s, j):
        part = rows_of(j * TOK, TOK)
        whole[part, :HD] = (dkv[s % 2, part, :HD] * SCALE).astype(BF16)
        whole[part, HD:] = dkv[s % 2, part, HD:].astype(BF16)

        def add(arrived):
            whole[part, :HD] = (dkv[s % 2, part, :HD] * SCALE + arrived[:, :HD].astype(F32)).astype(BF16)
            whole[part, HD:] = (dkv[s % 2, part, HD:] + arrived[:, HD:].astype(F32)).astype(BF16)

        @pl.when((z <= NZ - 2) & ((s >= 2) | (j == NX - 1)))
        def _():
            if s == 1:
                first.wait_recv()
                add(first_in[...])
            else:
                ring(s - 2, j).wait_recv()
                add(ring_in[s - 2, part, :])

        return part

    def pass_sums(s, j):
        part = summed(s, j)
        ring_out[s - 1, part, :] = whole[part, :]
        ring(s - 1, j).start()

    for s in range(1, WIN - 1):

        @pl.when(z >= WIN - 1 - s)
        def _():
            dkv[s % 2] = jnp.zeros((ROW, 2 * HD), F32)

            def one(a, _):
                backward_tile(s, a, ROW)
                if s >= 2:

                    @pl.when(z >= WIN - s)
                    def _():
                        pass_sums(s - 1, a)

                return 0

            lax.fori_loop(0, NX, one, 0)

    dkv[(WIN - 1) % 2] = jnp.zeros((ROW, 2 * HD), F32)

    def end(i, _):
        a = (x + i + 1) % NX
        for c in range(NX):

            @pl.when(a == c)
            def _():
                backward_tile(WIN - 1, c, (c + 1) * TOK)

        kept = keep[rows_of(a * TOK, TOK), :]
        value = acc_t[a] * SCALE
        for r in range(REP):
            piece = value[:, r * HD : (r + 1) * HD].T.astype(BF16)
            q_s[a, r * HD : (r + 1) * HD, :] = piece
            dq[a, :, r * HD : (r + 1) * HD] = (piece.astype(F32) * kept).astype(BF16)
        send_turn(i, 7, dq, text_grad.at[:, cols(x * QC, QC)])

        @pl.when(z >= 1)
        def _():
            pass_sums(WIN - 2, i)

        return 0

    lax.fori_loop(0, NX, end, 0)

    def z_pieces(peer):
        return [
            (scatq.at[rows_of(peer * 32, 32)], rxq.at[z]),
            (scatkv.at[rows_of(peer * 32, 32)], rxkv.at[z]),
            (vec_z, r_z.at[z]),
        ]

    own_z = [pltpu.make_async_copy(src, dst, own_sem.at[12 + k]) for k, (src, dst) in enumerate(z_pieces(z))]
    sent_z = []
    for d in range(1, NZ):
        peer = (z + d) % NZ
        sent_z.append([
            remote(src, dst, z_send.at[d - 1, k], z_recv.at[d - 1, k], ctx_of(peer, x))
            for k, (src, dst) in enumerate(z_pieces(peer))
        ])

    def send_z(k):
        for d in (3, 2, 4, 1, 5, 0, 6):
            sent_z[d][k].start()
        own_z[k].start()

    def arrived_z(k):
        own_z[k].wait()
        for d in range(NZ - 1):
            sent_z[d][k].wait_recv()

    vec[...] = jnp.zeros_like(vec)
    for r in range(REP):
        at = slice(r * HD, (r + 1) * HD)
        grads = jnp.concatenate([q_s[a, at, :] for a in range(NX)], axis=0)
        scattered = jnp.dot(onehot_t[...], grads, preferred_element_type=F32)
        scatq[:, at] = scattered.astype(BF16)
        vec[r : r + 1, :] = jnp.sum(scattered * raw[:, at].astype(F32), axis=0, keepdims=True)
        vec[10 + r : 11 + r, :] = jnp.sum(scattered, axis=0, keepdims=True)
    send_z(0)

    for i in range(NX):
        j = (x + i + 1) % NX
        part = summed(WIN - 1, j)
        kept = keep[part, :]
        mkv[part, :HD] = (whole[part, :HD].astype(F32) * kept).astype(BF16)
        mkv[part, HD:] = (whole[part, HD:].astype(F32) * kept).astype(BF16)
        for k in (8, 9):
            if i < NX - 1:
                sent_x[i][k].start()
            else:
                own_x[k].start()
    scattered = jnp.dot(onehot_t[...], whole[...], preferred_element_type=F32)
    scatkv[...] = scattered.astype(BF16)
    send_z(1)
    scale_part = jnp.sum(scattered * raw[:, QC:].astype(F32), axis=0, keepdims=True)
    shift_part = jnp.sum(scattered, axis=0, keepdims=True)
    for k in range(2):
        vec[REP + k : REP + k + 1, :] = scale_part[:, k * HD : (k + 1) * HD]
        vec[10 + REP + k : 11 + REP + k, :] = shift_part[:, k * HD : (k + 1) * HD]
    own_dp = pltpu.make_async_copy(vec, r_dp.at[dp], own_sem.at[15])
    sent_dp = [
        remote(vec, r_dp.at[dp], dp_send.at[d - 1], dp_recv.at[d - 1], {"dp": (dp + d) % NDP}) for d in range(1, NDP)
    ]
    for copy in sent_dp:
        copy.start()
    own_dp.start()

    own_dp.wait()
    for copy in sent_dp:
        copy.wait_recv()
    value = r_dp[0]
    for k in range(1, NDP):
        value = value + r_dp[k]
    vec_z[...] = value
    send_z(2)

    arrived_z(0)
    arrived_z(1)
    slots_q = rxq[0].astype(F32)
    slots_kv = rxkv[0].astype(F32)
    for k in range(1, NZ):
        slots_q = slots_q + rxq[k].astype(F32)
        slots_kv = slots_kv + rxkv[k].astype(F32)
    grad = jnp.concatenate([slots_q, slots_kv], axis=1) * scale
    for k in range(NX):
        piece = grad[k * SLOTS : (k + 1) * SLOTS]
        igs[k] = jnp.concatenate([piece[:, :HALF], piece[:, HALF:]], axis=0).astype(BF16)
    send_x(10)

    arrived_z(2)
    value = r_z[0]
    for k in range(1, NZ):
        value = value + r_z[k]
    vec_x[...] = value
    send_x(11)
    arrived_x(11)
    for head in range(NX):
        for out, at in ((scale_out, 0), (shift_out, 10)):
            out[head * REP : (head + 1) * REP, :] = r_x[head, at : at + REP, :]
            out[NX * REP + head : NX * REP + head + 1, :] = r_x[head, at + REP : at + REP + 1, :]
            out[NX * (REP + 1) + head : NX * (REP + 1) + head + 1, :] = r_x[head, at + REP + 1 : at + REP + 2, :]
    arrived_x(10)
    for head in range(NX):
        key, val = NX * QC + head * HD, NX * (QC + HD) + head * HD
        both = image_out[head].astype(F32)
        both = jnp.concatenate([both[:SLOTS], both[SLOTS:]], axis=1).astype(BF16)
        image_grad[:, head * QC : (head + 1) * QC] = both[:, :QC]
        image_grad[:, key : key + HD] = both[:, QC : QC + HD]
        image_grad[:, val : val + HD] = both[:, QC + HD :]
    for k in range(6, 10):
        arrived_x(k)

    for k in range(4):

        @pl.when((z >= k) & (z <= NZ - 2))
        def _():
            for j in range(NX):
                if k == 0:
                    key_step(j, 0).wait_send()
                    key_step(j, 1).wait_send()
                else:
                    hop(k, j).wait_send()

        @pl.when(z >= k + 1)
        def _():
            for j in range(NX):
                ring(3 - k, j).wait_send()

    @pl.when((z >= 4) & (z <= NZ - 2))
    def _():
        hop(4, NX - 1).wait_send()

    @pl.when(z >= WIN - 1)
    def _():
        first.wait_send()

    for k in range(2):
        for d in range(NX):
            image_step(up, 0, d, k).wait_send()
            image_step(down, 1, d, k).wait_send()
    for group in sent_x + sent_z + ups[1:] + downs[1:]:
        for copy in group:
            copy.wait_send()
    for copy in sent_dp:
        copy.wait_send()


def land_kernel(*refs):
    half = len(refs) // 2
    sems = refs[-1]
    copies = [pltpu.make_async_copy(refs[k], refs[half + k], sems.at[k]) for k in range(half)]
    for copy in copies:
        copy.start()
    for copy in copies:
        copy.wait()


def shape(dims, kind):
    return jax.ShapeDtypeStruct(dims, kind)


ANY = pl.BlockSpec(memory_space=pl.ANY)
VMEM = pl.BlockSpec(memory_space=pltpu.VMEM)
DMA = pltpu.SemaphoreType.DMA
LIMIT = 60 * 1024 * 1024


def per_device(
    text_rows, image_rows, tile_counts, tile_offsets, doc_ids, out_grad, proj_scale, proj_shift
):
    attn_out, text_grad, image_grad, scale_grad, shift_grad = pl.pallas_call(
        layer_kernel,
        out_shape=(
            shape((TOK, NX * QC), BF16),
            shape((TOK, NX * HC), BF16),
            shape((SLOTS, NX * HC), BF16),
            shape((NX * HC // HD, HD), F32),
            shape((NX * HC // HD, HD), F32),
        ),
        in_specs=[ANY, ANY] + [VMEM] * 6,
        out_specs=(ANY, ANY, VMEM, VMEM, VMEM),
        scratch_shapes=[
            pltpu.VMEM((NX, 16, HALF), BF16),
            pltpu.VMEM((8, TOK), jnp.int32),
            pltpu.VMEM((NX, 16, HALF), BF16),
            pltpu.VMEM((NX, TOK, QC), BF16),
            pltpu.VMEM((NX, TOK, QC), BF16),
            pltpu.VMEM((WIN, ROW, 2 * HD), BF16),
            pltpu.VMEM((NZ * NX, 16, HALF), BF16),
            pltpu.VMEM((NZ * NX, 8, TOK), jnp.int32),
            pltpu.VMEM((NSLOT, HC), BF16),
            pltpu.VMEM((NSLOT, HC), BF16),
            pltpu.VMEM((NSLOT, ROW), BF16),
            pltpu.VMEM((ROW, HD), F32),
            pltpu.VMEM((NX, 2 * HD, LANES), BF16),
            pltpu.VMEM((NX, HD, LANES), BF16),
            pltpu.VMEM((NX, LANES, HD), BF16),
            pltpu.VMEM((NX, LANES, HD), BF16),
            pltpu.VMEM((WIN, ROW, 2 * HD), BF16),
            pltpu.VMEM((WIN, ROW, HD), BF16),
            pltpu.VMEM((WIN, HD, ROW), BF16),
            pltpu.VMEM((WIN, HD, ROW), BF16),
            pltpu.VMEM((WIN - 1, NX, ROW, LANES), BF16),
            pltpu.VMEM((TOK, LANES), BF16),
            pltpu.VMEM((NX, HD, LANES), F32),
            pltpu.VMEM((NX, 1, LANES), F32),
            pltpu.VMEM((NX, 1, LANES), F32),
            pltpu.VMEM((WIN, NX, 1, LANES), F32),
            pltpu.VMEM((NX, 1, LANES), F32),
            pltpu.VMEM((2, ROW, 2 * HD), F32),
            pltpu.VMEM((NX, TOK, QC), BF16),
            pltpu.VMEM((NX, TOK, QC), BF16),
            pltpu.VMEM((TOK, 2 * HD), BF16),
            pltpu.VMEM((TOK, 2 * HD), BF16),
            pltpu.VMEM((4, ROW, 2 * HD), BF16),
            pltpu.VMEM((4, ROW, 2 * HD), BF16),
            pltpu.VMEM((ROW, 2 * HD), BF16),
            pltpu.VMEM((ROW, 2 * HD), BF16),
            pltpu.VMEM((NSLOT, QC), BF16),
            pltpu.VMEM((NSLOT, 2 * HD), BF16),
            pltpu.VMEM((NZ, 32, QC), BF16),
            pltpu.VMEM((NZ, 32, 2 * HD), BF16),
            pltpu.VMEM((NX, 16, HALF), BF16),
            pltpu.VMEM((24, HD), F32),
            pltpu.VMEM((24, HD), F32),
            pltpu.VMEM((24, HD), F32),
            pltpu.VMEM((NDP, 24, HD), F32),
            pltpu.VMEM((NZ, 24, HD), F32),
            pltpu.VMEM((NX, 24, HD), F32),
            DMA((2, 4, 2)), DMA((2, 4, 2)), DMA((4, 2)), DMA((4, 2)),
            DMA((16,)), DMA((3, 12)), DMA((3, 12)), DMA((5, 4)), DMA((5, 4)),
            DMA((3, 2)), DMA((3, 2)), DMA((4, 2)), DMA((4, 2)),
            DMA((5, 4)), DMA((5, 4)), DMA((7, 3)), DMA((7, 3)), DMA((7,)), DMA((7,)),
        ],
        compiler_params=pltpu.CompilerParams(
            collective_id=0, has_side_effects=True, vmem_limit_bytes=LIMIT
        ),
        name="layer",
    )(
        text_rows[0], out_grad[0], image_rows[0], tile_counts, tile_offsets, doc_ids,
        proj_scale.reshape(NX * HC // HD, HD), proj_shift.reshape(NX * HC // HD, HD),
    )
    results = (attn_out, text_grad, image_grad, scale_grad, shift_grad)
    attn_out, text_grad, image_grad, scale_grad, shift_grad = pl.pallas_call(
        land_kernel,
        out_shape=tuple(shape(a.shape, a.dtype) for a in results),
        in_specs=[VMEM] * 5,
        out_specs=(ANY,) * 5,
        scratch_shapes=[DMA((5,))],
        name="land",
    )(*results)
    return (
        attn_out[None], text_grad[None], image_grad[None],
        scale_grad.reshape(NX * HC), shift_grad.reshape(NX * HC),
    )


def solution(mesh):
    return jax.shard_map(
        per_device,
        mesh=mesh,
        in_specs=(
            P("dp", "ctx", None),
            P("dp", "ctx", None),
            P("dp", "ctx"),
            P("dp", "ctx"),
            P("dp", "ctx"),
            P("dp", "ctx", None),
            P(),
            P(),
        ),
        out_specs=(P("dp", "ctx", None), P("dp", "ctx", None), P("dp", "ctx", None), P(), P()),
        check_vma=False,
    )
```
